32 devices in a mesh: dp: 8 (over z, x), rep: 4 (over y, core).
Axes of the slice: x: 2, y: 2, z: 4, core: 2. Of those that a mesh axis runs over, the one named last changes fastest.
Arguments:
- tokens: bfloat16 [32, 1024, 1024], P(('dp', 'rep')), may hold values from -40 to 40
- segment_ids: int32 [32, 1024], P(('dp', 'rep')), may hold values from 0 to 3, never falling along the last dimension, each value on 1 to 512 neighbouring positions
- cotangent: bfloat16 [32, 1024, 1024], P(('dp', 'rep')), may hold values from -12 to 12
- qkv_weight: float32 [1024, 3072], P('dp'), may hold values from -0.09375 to 0.09375
- out_weight: float32 [1024, 1024], P('dp'), may hold values from -0.5 to 0.5
- up_weight: float32 [1024, 4096], P('dp'), may hold values from -0.09375 to 0.09375
- down_weight: float32 [1024, 4096], P('dp'), may hold values from -0.09375 to 0.09375
- vectors: float32 [12, 1024], P(None, 'dp'), may hold values from -1.3 to 7.5, as said below
- qkv_first: float32 [1024, 3072], P('dp'), may hold values from -0.00030517578 to 0.00030517578
- qkv_second: float32 [1024, 3072], P('dp'), may hold values from 1.2683868e-08 to 5.0544738e-08
- out_first: float32 [1024, 1024], P('dp'), may hold values from -5.340576e-05 to 5.340576e-05
- out_second: float32 [1024, 1024], P('dp'), may hold values from 3.2424927e-10 to 1.2969971e-09
- up_first: float32 [1024, 4096], P('dp'), may hold values from -0.00010681152 to 0.00010681152
- up_second: float32 [1024, 4096], P('dp'), may hold values from 1.2111664e-09 to 4.863739e-09
- down_first: float32 [1024, 4096], P('dp'), may hold values from -0.00010681152 to 0.00010681152
- down_second: float32 [1024, 4096], P('dp'), may hold values from 1.4591217e-09 to 5.817413e-09
- vectors_first: float32 [12, 1024], P(None, 'dp'), may hold values from -0.00015258789 to 0.00015258789
- vectors_second: float32 [12, 1024], P(None, 'dp'), may hold values from 3.1471252e-09 to 1.2397766e-08
Outputs:
- block_out: float32 [32, 1024, 1024], P(('dp', 'rep'))
- input_grad: float32 [32, 1024, 1024], P(('dp', 'rep'))
- grad_norm: float32 [], replicated
- input_scale: float32 [], replicated
- qkv_next: float32 [1024, 3072], P('dp')
- out_next: float32 [1024, 1024], P('dp')
- up_next: float32 [1024, 4096], P('dp')
- down_next: float32 [1024, 4096], P('dp')
- vectors_next: float32 [12, 1024], P(None, 'dp')
- qkv_first_next: float32 [1024, 3072], P('dp')
- out_first_next: float32 [1024, 1024], P('dp')
- up_first_next: float32 [1024, 4096], P('dp')
- down_first_next: float32 [1024, 4096], P('dp')
- vectors_first_next: float32 [12, 1024], P(None, 'dp')
- qkv_second_next: float32 [1024, 3072], P('dp')
- out_second_next: float32 [1024, 1024], P('dp')
- up_second_next: float32 [1024, 4096], P('dp')
- down_second_next: float32 [1024, 4096], P('dp')
- vectors_second_next: float32 [12, 1024], P(None, 'dp')
- qkv_half: bfloat16 [1024, 3072], P('dp')
- out_half: bfloat16 [1024, 1024], P('dp')
- up_half: bfloat16 [1024, 4096], P('dp')
- down_half: bfloat16 [1024, 4096], P('dp')
- vectors_half: bfloat16 [12, 1024], P(None, 'dp')
The draws below stay inside these ranges and needn't reach their ends.
Inputs may be any that keep to these rules, and one draw needn't show every extreme that they name: `segment_ids`: ids never fall along a row; every row holds all 4 documents, each of 1 to 512 tokens, one of exactly 512. `vectors`: gains are positive.
All inputs are finite; a program needn't handle non-finite values.
Results may differ from the reference program's by a relative error of at most 0.012.
The reference program's roundings to bfloat16 on the way count: a program that leaves them out, or rounds other values in their place, can miss the bound.
Values may be sent and summed in bfloat16 or wider, within the bound.
No kernel may reach another device: no remote copies, remote signals or barrier semaphores. Data moves between devices by JAX's collectives and lax.ppermute only.
A program may use at most 320 MiB of HBM per device.

```python
import math
from functools import reduce
import jax
import jax.numpy as jnp
import numpy as np
from jax import lax

HEADS = 16
HEAD_DIM = 64
D = 1024
FF = 4096
VECS = 12
LEN = 1024
SEQS_DEV = 1
DOCS = 4
STEP = 10
ROWS = 32
N_DP = 8
N_REP = 4


def draw_tokens(key, part):
    dims_all = (ROWS, LEN, D)
    values = jnp.clip(jax.random.normal(key, dims_all, jnp.float32), -4.0, 4.0)
    dp_rise = math.log(3.0)
    row_ids = jnp.arange(ROWS, dtype=jnp.int32)
    device = row_ids // SEQS_DEV
    along_dp = (device // N_REP).astype(jnp.float32) / max(N_DP - 1, 1)
    along_rep = (device % N_REP).astype(jnp.float32) / max(N_REP - 1, 1)
    factor = jnp.exp(dp_rise * along_dp + math.log(3.0) * along_rep)
    return (values * factor[:, None, None]).astype(jnp.bfloat16)


def draw_cotangent(key, part):
    dims_all = (ROWS, LEN, D)
    values = jnp.clip(jax.random.normal(key, dims_all, jnp.float32), -4.0, 4.0)
    rise = math.log(3.0)
    columns = jnp.arange(D, dtype=jnp.float32) / max(D - 1, 1)
    return (values * jnp.exp(rise * columns)[None, None, :]).astype(jnp.bfloat16)


def draw_vectors(key, part):
    first_key, second_key = jax.random.split(key, 2)
    columns = jnp.arange(D, dtype=jnp.float32) / max(D - 1, 1)
    ramp = jnp.exp(math.log(3.0) * columns)
    biases = 0.3 * jnp.clip(jax.random.normal(second_key, (VECS, D), jnp.float32), -4.0, 4.0)
    rough = jnp.exp(jax.random.uniform(first_key, (VECS, D), jnp.float32, math.log(0.7), math.log(1.4)))
    row_ids = jnp.arange(VECS, dtype=jnp.int32)
    is_gain = (row_ids == 0) | (row_ids == 5)
    return jnp.where(is_gain[:, None], ramp[None, :] * rough, biases)


def block_scale(rng, extent, cuts, least, largest):
    level, own = 1.0, jax.random.fold_in(rng, 6)
    for axis_at, blocks in cuts:
        heights = jnp.exp(jax.random.uniform(jax.random.fold_in(own, axis_at), (blocks,), jnp.float32, least / len(cuts), largest / len(cuts)))
        level = level * jnp.repeat(heights, extent[axis_at] // blocks).reshape([-1 if axis == axis_at else 1 for axis in range(len(extent))])
    return level


def split_up(count, total, most, skew):
    loads = [(1 << 20) // math.isqrt(standing ** skew) + 1 for standing in range(2, count + 1)]
    rest, counts = total - most - (count - 1), [1] * (count - 1)
    while rest > 0:
        candidates = [i for i in range(count - 1) if counts[i] < most]
        pool, budget = sum([loads[i] for i in candidates]), rest
        for i in candidates:
            addition = min(most - counts[i], max(1, budget * loads[i] // pool), rest)
            counts[i] = counts[i] + addition
            rest = rest - addition
    return np.array([most] + counts)


def uneven(own_key, count, total, reach, skew):
    if count == 2:
        one = jax.random.randint(own_key, (), max(1, total - reach), min(reach, total - 1) + 1)
        return jnp.stack([one, total - one])
    lengths = jnp.asarray(split_up(count, total, reach, skew), jnp.int32)
    pairs = (count - 1) // 2
    donor, receiver = lengths[1:1 + 2 * pairs:2], lengths[2:2 + 2 * pairs:2]
    slack = jnp.minimum(donor - 1, reach - receiver)
    moved = jax.random.randint(jax.random.fold_in(own_key, 1), (pairs,), 0, 1 << 20) % (slack + 1)
    lengths = lengths.at[1:1 + 2 * pairs:2].set(donor - moved).at[2:2 + 2 * pairs:2].set(receiver + moved)
    return lengths[jax.random.permutation(jax.random.fold_in(own_key, 2), count)]


def scatter_about(key, shape, width, bound, shards=(), kind=jnp.bfloat16):
    entries = width * jax.random.normal(key, shape, jnp.float32)
    if shards:
        entries = entries * block_scale(key, shape, shards, -0.22, 0.18)
    return jnp.clip(entries, -bound, bound).astype(kind)


def setup_inputs(seed: int = 0) -> dict:
    arg_keys = jax.random.split(jax.random.key(seed), 19)
    tokens = draw_tokens(jax.random.fold_in(arg_keys[18], 71), 0)
    segment_ids = jax.vmap(lambda own: jnp.searchsorted(jnp.cumsum(uneven(own, DOCS, LEN, LEN // 2, 2)), jnp.arange(LEN), side="right"))(jax.random.split(arg_keys[1], ROWS)).reshape((ROWS, LEN)).astype(jnp.int32)
    cotangent = draw_cotangent(jax.random.fold_in(arg_keys[18], 71), 0)
    qkv_weight = scatter_about(arg_keys[3], (D, 3 * D), (4 * D) ** -0.5, 0.09375, ((0, 8),), jnp.float32)
    out_weight = scatter_about(arg_keys[4], (D, D), (D // 8) ** -0.5, 0.5, ((0, 8),), jnp.float32)
    up_weight = scatter_about(arg_keys[5], (D, FF), (4 * D) ** -0.5, 0.09375, ((0, 8),), jnp.float32)
    down_weight = scatter_about(arg_keys[6], (D, FF), FF ** -0.5, 0.09375, ((0, 8),), jnp.float32)
    vectors = draw_vectors(jax.random.fold_in(arg_keys[18], 71), 0)
    qkv_first = scatter_about(arg_keys[8], (D, 3 * D), (0.055 / D), 0.00030517578, ((0, 8),), jnp.float32)
    qkv_second = jnp.clip(jnp.exp(math.log(5.054473817267535e-08) - 1.38252788 * jax.random.uniform(arg_keys[9], (D, 3 * D), jnp.float32) ** block_scale(arg_keys[9], (D, 3 * D), ((0, 8),), -0.2, 0.2)), 1.2683868177987279e-08, 5.054473817267535e-08)
    out_first = scatter_about(arg_keys[10], (D, D), (0.0088 / D), 5.340576171875e-05, ((0, 8),), jnp.float32)
    out_second = jnp.clip(jnp.exp(math.log(1.2969970653031737e-09) - 1.3862944 * jax.random.uniform(arg_keys[11], (D, D), jnp.float32) ** block_scale(arg_keys[11], (D, D), ((0, 8),), -0.2, 0.2)), 3.2424926632579343e-10, 1.2969970653031737e-09)
    up_first = scatter_about(arg_keys[12], (D, FF), (0.017 / D), 0.00010681152, ((0, 8),), jnp.float32)
    up_second = jnp.clip(jnp.exp(math.log(4.863739189175931e-09) - 1.39022367 * jax.random.uniform(arg_keys[13], (D, FF), jnp.float32) ** block_scale(arg_keys[13], (D, FF), ((0, 8),), -0.2, 0.2)), 1.2111663894032176e-09, 4.863739189175931e-09)
    down_first = scatter_about(arg_keys[14], (D, FF), (0.019 / D), 0.00010681152, ((0, 8),), jnp.float32)
    down_second = jnp.clip(jnp.exp(math.log(5.817413217812373e-09) - 1.383021 * jax.random.uniform(arg_keys[15], (D, FF), jnp.float32) ** block_scale(arg_keys[15], (D, FF), ((0, 8),), -0.2, 0.2)), 1.4591217123438582e-09, 5.817413217812373e-09)
    vectors_first = scatter_about(arg_keys[16], (VECS, D), (0.0275 / D), 0.00015258789, ((1, 8),), jnp.float32)
    vectors_second = jnp.clip(jnp.exp(math.log(1.2397766369076635e-08) - 1.3710269 * jax.random.uniform(arg_keys[17], (VECS, D), jnp.float32) ** block_scale(arg_keys[17], (VECS, D), ((1, 8),), -0.2, 0.2)), 3.1471252270875993e-09, 1.2397766369076635e-08)
    return dict(tokens=tokens, segment_ids=segment_ids, cotangent=cotangent, qkv_weight=qkv_weight, out_weight=out_weight, up_weight=up_weight, down_weight=down_weight, vectors=vectors, qkv_first=qkv_first, qkv_second=qkv_second, out_first=out_first, out_second=out_second, up_first=up_first, up_second=up_second, down_first=down_first, down_second=down_second, vectors_first=vectors_first, vectors_second=vectors_second)


@jax.custom_vjp
def low(v):
    return lax.optimization_barrier(v.astype(jnp.bfloat16)).astype(jnp.float32)

@jax.custom_vjp
def low_back(v):
    return v

def low_keep(v):
    return (low(v), None)

def low_pass(kept, grad):
    return (grad,)

def back_keep(v):
    return (v, None)

def back_low(kept, grad):
    return (low(grad),)
low.defvjp(low_keep, low_pass)
low_back.defvjp(back_keep, back_low)
LN_EPS = 1e-05
CLIP_NORM = 1.0
BETA_ONE = 0.9
BETA_TWO = 0.95
ADAM_EPS = 1e-08
MATRIX_RATE = 0.1
VECTOR_RATE = 1.0
DECAY = 0.1
MASKED = -1e+30
HIGH = lax.Precision.HIGHEST

def norm_rows(values, gain_row, bias_row):
    centre = lax.optimization_barrier(jnp.mean(values, axis=-1, keepdims=True))
    shifted = values - centre
    spread = lax.optimization_barrier(jnp.mean(shifted * shifted, axis=-1, keepdims=True))
    return shifted * lax.rsqrt(spread + LN_EPS) * gain_row + bias_row

def attend(queries, key_rows, value_rows, segments):
    groups = segments.shape[0]
    block_rows = min(512, LEN)
    slopes = 2.0 ** (-8.0 * (jnp.arange(HEADS, dtype=jnp.float32) + 1.0) / HEADS)
    places = jnp.arange(LEN, dtype=jnp.int32)
    inv_root = 1.0 / math.sqrt(HEAD_DIM)

    def one_block(block_index):
        first_row = (block_index * block_rows).astype(jnp.int32)
        query_block = lax.dynamic_slice_in_dim(queries, first_row, block_rows, 2)
        query_segs = lax.dynamic_slice_in_dim(segments, first_row, block_rows, 1)
        query_places = first_row + jnp.arange(block_rows, dtype=jnp.int32)
        raw_dot = low_back(jnp.einsum('ghqd,ghkd->ghqk', query_block, key_rows, precision=HIGH))
        distance = (query_places[:, None] - places[None, :]).astype(jnp.float32)
        scores = raw_dot * inv_root - slopes[None, :, None, None] * distance[None, None]
        allowed = (places[None, None, :] <= query_places[None, :, None]) & (query_segs[:, :, None] == segments[:, None, :])
        scores = jnp.where(allowed[:, None], scores, MASKED)
        row_top = lax.optimization_barrier(jnp.max(scores, axis=-1, keepdims=True))
        weights = jnp.exp(scores - row_top)
        weights = weights / lax.optimization_barrier(jnp.sum(weights, axis=-1, keepdims=True))
        return jnp.einsum('ghqk,ghkd->ghqd', low(weights), value_rows, precision=HIGH)
    blocks = lax.map(jax.checkpoint(one_block), jnp.arange(LEN // block_rows, dtype=jnp.int32))
    return blocks.transpose(1, 2, 0, 3, 4).reshape(groups, HEADS, LEN, HEAD_DIM)

def forward(params, rows_in, segments):
    qkv_w, out_w, up_w, down_w, vec_low = [low(t) for t in params]
    groups = segments.shape[0]
    total_rows = groups * LEN
    up_rows = FF // D
    rows_flat = rows_in.reshape(total_rows, D)
    normed = low(norm_rows(rows_flat, vec_low[0], vec_low[1]))
    projected = jnp.dot(normed, qkv_w, precision=HIGH)
    queries = low(low_back(projected[:, :D] + vec_low[2]))
    key_rows = low(low_back(projected[:, D:2 * D]))
    value_rows = low(low_back(projected[:, 2 * D:] + vec_low[3]))

    def heads_first(t):
        return t.reshape(groups, LEN, HEADS, HEAD_DIM).transpose(0, 2, 1, 3)
    context = attend(heads_first(queries), heads_first(key_rows), heads_first(value_rows), segments)
    context = low(low_back(context.transpose(0, 2, 1, 3).reshape(total_rows, D)))
    branch = low_back(jnp.dot(context, out_w.T, precision=HIGH) + vec_low[4])
    middle = rows_flat + branch
    normed_two = low(norm_rows(middle, vec_low[5], vec_low[6]))
    hidden = low_back(jnp.dot(normed_two, up_w, precision=HIGH) + vec_low[7:7 + up_rows].reshape(FF))
    active = low(jax.nn.gelu(hidden, approximate=True))
    result = middle + low_back(jnp.dot(active, down_w.T, precision=HIGH) + vec_low[7 + up_rows])
    return result.reshape(groups, LEN, D)

def adam_step(weight, grad, first, second, rate, decay):
    first_next = BETA_ONE * first + (1.0 - BETA_ONE) * grad
    second_next = BETA_TWO * second + (1.0 - BETA_TWO) * grad * grad
    first_hat = first_next / (1.0 - BETA_ONE ** STEP)
    second_hat = second_next / (1.0 - BETA_TWO ** STEP)
    weight_next = weight - rate * (first_hat / (jnp.sqrt(second_hat) + ADAM_EPS) + decay * weight)
    return (weight_next, first_next, second_next)

def reference(tokens, segment_ids, cotangent, qkv_weight, out_weight, up_weight, down_weight, vectors, qkv_first, qkv_second, out_first, out_second, up_first, up_second, down_first, down_second, vectors_first, vectors_second):
    params = (qkv_weight, out_weight, up_weight, down_weight, vectors)
    group = math.gcd(ROWS, max(1, 4096 // LEN))
    step_count = ROWS // group
    rows_all = tokens.astype(jnp.float32)
    rows_split = rows_all.reshape(step_count, group, LEN, D)
    cot_split = cotangent.astype(jnp.float32).reshape(step_count, group, LEN, D)
    seg_split = segment_ids.reshape(step_count, group, LEN)
    starts = tuple((jnp.zeros(t.shape, jnp.float32) for t in params))

    def one_group(totals, item):
        rows_part, cot_part, seg_part = item
        result, pullback = jax.vjp(lambda weights_in, rows_x: forward(weights_in, rows_x, seg_part), params, rows_part)
        grads, row_grad = pullback(cot_part)
        return (tuple((a + b for a, b in zip(totals, grads))), (result, row_grad))
    grads, (outs_split, grads_split) = lax.scan(one_group, starts, (rows_split, cot_split, seg_split))
    block_out = outs_split.reshape(ROWS, LEN, D)
    input_grad = grads_split.reshape(ROWS, LEN, D)
    rows_flat = rows_all.reshape(ROWS * LEN, D)
    centre = lax.optimization_barrier(jnp.mean(rows_flat, axis=-1, keepdims=True))
    shifted = rows_flat - centre
    spread = lax.optimization_barrier(jnp.mean(shifted * shifted, axis=-1))
    input_scale = jnp.mean(jnp.sqrt(spread + LN_EPS))
    grad_norm = jnp.sqrt(reduce(lambda a, b: a + b, [jnp.sum(g * g) for g in grads]))
    clip_factor = jnp.minimum(1.0, CLIP_NORM / (grad_norm + 1e-06))
    firsts = (qkv_first, out_first, up_first, down_first, vectors_first)
    seconds = (qkv_second, out_second, up_second, down_second, vectors_second)
    rates = (MATRIX_RATE, MATRIX_RATE, MATRIX_RATE, MATRIX_RATE, VECTOR_RATE)
    decays = (DECAY, DECAY, DECAY, DECAY, 0.0)
    nexts, first_nexts, second_nexts, halves = ([], [], [], [])
    for weight, grad, first, second, rate, decay in zip(params, grads, firsts, seconds, rates, decays):
        weight_next, first_next, second_next = adam_step(weight, grad * clip_factor, first, second, rate, decay)
        nexts.append(weight_next)
        first_nexts.append(first_next)
        second_nexts.append(second_next)
        halves.append(weight_next.astype(jnp.bfloat16))
    return (block_out, input_grad, grad_norm, input_scale, nexts[0], nexts[1], nexts[2], nexts[3], nexts[4], first_nexts[0], first_nexts[1], first_nexts[2], first_nexts[3], first_nexts[4], second_nexts[0], second_nexts[1], second_nexts[2], second_nexts[3], second_nexts[4], halves[0], halves[1], halves[2], halves[3], halves[4])
```

```python
from functools import partial
from functools import reduce
import math

import jax
import jax.numpy as jnp
from jax import lax
from jax.experimental import pallas as pl
from jax.experimental.pallas import tpu as pltpu
from jax.sharding import PartitionSpec as P

HEADS = 16
HEAD_DIM = 64
D = 1024
FF = 4096
STEP = 10


LN_EPS = 1e-05
CLIP_NORM = 1.0
BETA_ONE = 0.9
BETA_TWO = 0.95
ADAM_EPS = 1e-08
MATRIX_RATE = 0.1
VECTOR_RATE = 1.0
DECAY = 0.1
MASKED = -1e30

F32 = jnp.float32
BF16 = jnp.bfloat16
AXES = ("dp", "rep")
MIB = 2**20
NN = (((1,), (0,)), ((), ()))
NT = (((1,), (1,)), ((), ()))
TN = (((0,), (0,)), ((), ()))


def mxu(left, right, dims):
    return lax.dot_general(left, right, dims, preferred_element_type=F32)


def shape(dims, dtype):
    return jax.ShapeDtypeStruct(dims, dtype)


def settings(mib=56):
    return pltpu.CompilerParams(vmem_limit_bytes=mib * MIB)


SCALE = 50


def cost(flops, moved):
    return pl.CostEstimate(flops=int(SCALE * flops), bytes_accessed=int(SCALE * moved), transcendentals=0)


def swap(values, z=0, x=0, y=0, core=0):
    n_dp, n_rep = lax.axis_size("dp"), lax.axis_size("rep")
    dp_bits, rep_bits = 2 * z + x, 2 * y + core
    pairs = [
        (dp * n_rep + rep, (dp ^ dp_bits) * n_rep + (rep ^ rep_bits))
        for dp in range(n_dp)
        for rep in range(n_rep)
    ]
    return lax.ppermute(values, AXES, pairs)


def pack(own, place, parts, split_y):
    mine = []
    for low, core_step, width in parts:
        start = low + place[3] * core_step + (place[2] * width if split_y else 0)
        mine.append(lax.dynamic_slice_in_dim(own, start, width, 1))
    return mine[0] if len(mine) == 1 else jnp.concatenate(mine, axis=1)


def gathered(rows, stacks, column, width, target, half, y_step):
    return [
        (array, [(z, x, y, core, rows, column, width, target, half, y_step) for z in zs])
        for array, zs, x, y, core in stacks
    ]


def whole_rows(own):
    full = lax.all_gather(own, "dp", axis=0, tiled=True)
    return [(full, [(0, 0, 0, 0, full.shape[0], 0, full.shape[1], 0, 0, 0)])]


def piece_copies(place, ref, plan, target, sems, first):
    copies, at = [], None
    for i, (z, x, y, core, rows, column, width, start, half, y_step) in enumerate(plan):
        if len(ref.shape) == 3:
            row = pl.multiple_of(((place[0] ^ z) * 2 + (place[1] ^ x)) * rows, rows)
            at = start + (place[3] ^ core) * half + (place[2] ^ y) * y_step
            column_at = pl.multiple_of(at, 128)
            source = ref.at[i, pl.ds(0, rows), pl.ds(column, width)]
        else:
            row, column_at, source = 0, start, ref
        copies.append(
            pltpu.make_async_copy(
                source, target.at[pl.ds(row, rows), pl.ds(column_at, width)], sems.at[first + i]
            )
        )
    return at, copies


def turned_step(place, steps):
    half = steps // 2
    return lambda i, *_: lax.rem((1 - place[3]) * half + i, steps)


QUERY_BLOCK = 128
KEY_SPAN = 512


def bands(length):
    return [
        (b * QUERY_BLOCK, max(0, b * QUERY_BLOCK - KEY_SPAN), (b + 1) * QUERY_BLOCK)
        for b in range(length // QUERY_BLOCK)
    ]


def head_slope(head):
    return jnp.exp2(-8.0 * (head.astype(F32) + 1.0) / HEADS)


def head_lanes(h):
    lane = lax.broadcasted_iota(jnp.int32, (1, 2 * HEAD_DIM), 1)
    return (lane >= HEAD_DIM) if h else (lane < HEAD_DIM)


def both_heads(rows):
    return jnp.concatenate([jnp.where(head_lanes(h), rows, BF16(0)) for h in range(2)], axis=0)


def own_lanes(rows):
    half = rows.shape[0] // 2
    return jnp.where(head_lanes(0), rows[:half], rows[half:])


def fill_base(segs_row, segs_column, base, length):
    for b, (first, low, high) in enumerate(bands(length)):
        keys = low + lax.broadcasted_iota(jnp.int32, (high - low, QUERY_BLOCK), 0)
        rows = first + lax.broadcasted_iota(jnp.int32, (high - low, QUERY_BLOCK), 1)
        allowed = (keys <= rows) & (
            segs_column[low:high, :] == segs_row[:, first : first + QUERY_BLOCK]
        )
        base[b, : high - low, :] = jnp.where(allowed, (keys - rows).astype(F32), MASKED)


def biased(scores, base, pair):
    return jnp.concatenate(
        [
            scores[:, h * QUERY_BLOCK : (h + 1) * QUERY_BLOCK] + head_slope(2 * pair + h) * base
            for h in range(2)
        ],
        axis=1,
    )


def attend_forward_kernel(
    first_pair, segs_row, segs_column, q_ref, k_ref, v_ref, *refs
):
    c_ref, lse_ref, base = refs[-3:]
    length = q_ref.shape[0]

    @pl.when(pl.program_id(0) == 0)
    def _():
        fill_base(segs_row, segs_column, base, length)

    pair = first_pair + pl.program_id(0)
    for b, (first, low, high) in enumerate(bands(length)):
        rows = slice(first, first + QUERY_BLOCK)
        queries, keys, values = q_ref[rows, :], k_ref[low:high, :], v_ref[low:high, :]
        scaled = both_heads(queries * BF16(1.0 / math.sqrt(HEAD_DIM)))
        scores = biased(mxu(keys, scaled, NT), base[b, : high - low, :], pair)
        top = jnp.max(scores, axis=0, keepdims=True)
        weights = jnp.exp(scores - top)
        total = jnp.sum(weights, axis=0, keepdims=True)
        probs = (weights * (1.0 / total)).astype(BF16)
        c_ref[rows, :] = own_lanes(mxu(probs, values, TN)).astype(BF16)
        lse = top + jnp.log(total)
        for h in range(2):
            lse_ref[0, h : h + 1, rows] = lse[:, h * QUERY_BLOCK : (h + 1) * QUERY_BLOCK]


def attend_forward(qkv, segs, segs_column, first_pair, pairs, context=None):
    length, width = qkv.shape[0], 2 * HEAD_DIM
    per = D // width
    before = [] if context is None else [context]
    return pl.pallas_call(
        partial(attend_forward_kernel, first_pair),
        grid=(pairs,),
        in_specs=[
            pl.BlockSpec((1, length), lambda i: (0, 0)),
            pl.BlockSpec((length, 1), lambda i: (0, 0)),
            pl.BlockSpec((length, width), lambda i: (0, first_pair + i)),
            pl.BlockSpec((length, width), lambda i: (0, per + first_pair + i)),
            pl.BlockSpec((length, width), lambda i: (0, 2 * per + first_pair + i)),
        ]
        + [pl.BlockSpec(memory_space=pltpu.HBM)] * len(before),
        out_specs=[
            pl.BlockSpec((length, width), lambda i: (0, first_pair + i)),
            pl.BlockSpec((1, 2, length), lambda i: (i, 0, 0)),
        ],
        input_output_aliases={5: 0} if before else {},
        out_shape=[
            shape((length, D), BF16),
            shape((pairs, 2, length), F32),
        ],
        scratch_shapes=[pltpu.VMEM((length // QUERY_BLOCK, KEY_SPAN + QUERY_BLOCK, QUERY_BLOCK), F32)],
        compiler_params=settings(),
        cost_estimate=cost(3.5e9 * pairs, 1e6 * pairs),
        name="attend_forward",
    )(segs, segs_column, qkv, qkv, qkv, *before)


def attend_backward_kernel(
    first_pair,
    pairs,
    place,
    segs_row,
    segs_column,
    q_ref,
    k_ref,
    v_ref,
    g_ref,
    lse_ref,
    o_ref,
    send_ref,
    sums_ref,
    base,
    dk,
    dv,
):
    length = q_ref.shape[0]

    @pl.when(pl.program_id(0) == 0)
    def _():
        fill_base(segs_row, segs_column, base, length)

    pair = first_pair + turned_step(place, pairs)(pl.program_id(0))
    dk[...] = jnp.zeros_like(dk)
    dv[...] = jnp.zeros_like(dv)
    query_sum = jnp.zeros((1, 2 * HEAD_DIM), F32)
    inv_root = BF16(1.0 / math.sqrt(HEAD_DIM))
    for b, (first, low, high) in enumerate(bands(length)):
        rows = slice(first, first + QUERY_BLOCK)
        keys, values = k_ref[low:high, :], v_ref[low:high, :]
        queries, grads = both_heads(q_ref[rows, :]), both_heads(g_ref[rows, :])
        scores = biased(mxu(keys, queries * inv_root, NT), base[b, : high - low, :], pair)
        lse = jnp.concatenate([lse_ref[0, h : h + 1, rows] for h in range(2)], axis=1)
        probs = jnp.exp(scores - lse)
        prob_grad = mxu(values, grads * inv_root, NT)
        row_dot = jnp.sum(probs * prob_grad, axis=0, keepdims=True)
        score_grad = (probs * (prob_grad - row_dot)).astype(BF16)
        dv[low:high, :] += mxu(probs.astype(BF16), grads, NN)
        dk[low:high, :] += mxu(score_grad, queries, NN)
        dq = own_lanes(mxu(score_grad, keys, TN)).astype(BF16)
        o_ref[0, rows, :] = dq
        query_sum = query_sum + jnp.sum(dq.astype(F32), axis=0, keepdims=True)
    o_ref[1] = dk[...].astype(BF16)
    value_grad = dv[...].astype(BF16)
    o_ref[2] = value_grad
    sums_ref[0:1, :] = query_sum
    sums_ref[1:2, :] = jnp.sum(value_grad.astype(F32), axis=0, keepdims=True)

    @pl.when(pl.program_id(0) < pairs // 2)
    def _():
        send_ref[...] = o_ref[...]


def attend_backward(qkv, segs, segs_column, grads, lse, first_pair, pairs, place):
    length, width = qkv.shape[0], 2 * HEAD_DIM
    per = D // width

    def heads(first):
        return pl.BlockSpec(
            (length, width), lambda i, s: (0, first + first_pair + turned_step(s, pairs)(i))
        )

    return pl.pallas_call(
        partial(attend_backward_kernel, first_pair, pairs),
        grid_spec=pltpu.PrefetchScalarGridSpec(
            num_scalar_prefetch=1,
            grid=(pairs,),
            in_specs=[
                pl.BlockSpec((1, length), lambda i, s: (0, 0)),
                pl.BlockSpec((length, 1), lambda i, s: (0, 0)),
                heads(0),
                heads(per),
                heads(2 * per),
                heads(0),
                pl.BlockSpec((1, 2, length), lambda i, s: (turned_step(s, pairs)(i), 0, 0)),
            ],
            out_specs=[
                pl.BlockSpec((3, length, width), lambda i, s: (0, 0, turned_step(s, pairs)(i))),
                pl.BlockSpec((3, length, width), lambda i, s: (0, 0, jnp.minimum(i, pairs // 2 - 1))),
                pl.BlockSpec((2, width), lambda i, s: (0, turned_step(s, pairs)(i))),
            ],
            scratch_shapes=[
                pltpu.VMEM((length // QUERY_BLOCK, KEY_SPAN + QUERY_BLOCK, QUERY_BLOCK), F32),
                pltpu.VMEM((length, width), F32),
                pltpu.VMEM((length, width), F32),
            ],
        ),
        out_shape=[
            shape((3, length, pairs * width), BF16),
            shape((3, length, pairs * width // 2), BF16),
            shape((2, pairs * width), F32),
        ],
        compiler_params=settings(),
        cost_estimate=cost(5e9 * pairs, 1e6 * pairs),
        name="attend_backward",
    )(place, segs, segs_column, qkv, qkv, qkv, grads, lse)


ROW_BLOCK = 256


def row_stats(values):
    centre = jnp.mean(values, axis=-1, keepdims=True)
    shifted = values - centre
    spread = jnp.mean(shifted * shifted, axis=-1, keepdims=True)
    inverse = lax.rsqrt(spread + LN_EPS)
    return shifted * inverse, inverse, spread


def norm_back(upstream, scaled, inverse, gain_row):
    weighted = upstream * gain_row
    return inverse * (
        weighted
        - jnp.mean(weighted, axis=-1, keepdims=True)
        - scaled * jnp.mean(weighted * scaled, axis=-1, keepdims=True)
    )


def column_sum(values):
    return jnp.sum(values, axis=0, keepdims=True)


def accumulate(ref, values):
    step = pl.program_id(0)

    @pl.when(step == 0)
    def _():
        ref[...] = values

    @pl.when(step > 0)
    def _():
        ref[...] += values


def turn_kernel(g_ref, turned_ref, sum_ref):
    values = g_ref[...]
    turned_ref[...] = values.T
    accumulate(sum_ref, column_sum(values.astype(F32)))


def turn(cot):
    length, width = cot.shape
    return pl.pallas_call(
        turn_kernel,
        grid=(length // ROW_BLOCK,),
        in_specs=[pl.BlockSpec((ROW_BLOCK, width), lambda i: (i, 0))],
        out_specs=[
            pl.BlockSpec((width, ROW_BLOCK), lambda i: (0, i)),
            pl.BlockSpec((1, width), lambda i: (0, 0)),
        ],
        out_shape=[shape((width, length), BF16), shape((1, width), F32)],
        compiler_params=settings(),
        cost_estimate=cost(0, 8e6),
        name="turn",
    )(cot)


def first_norm_kernel(x_ref, vec_ref, h_ref, turned_ref, scale_ref):
    scaled, _, spread = row_stats(x_ref[...].astype(F32))
    normed = (scaled * vec_ref[0:1, :] + vec_ref[1:2, :]).astype(BF16)
    h_ref[...] = normed
    turned_ref[...] = normed.T
    accumulate(scale_ref, jnp.broadcast_to(column_sum(jnp.sqrt(spread + LN_EPS)), (1, 128)))


def first_norm(rows, vec):
    length, width = rows.shape
    return pl.pallas_call(
        first_norm_kernel,
        grid=(length // ROW_BLOCK,),
        in_specs=[
            pl.BlockSpec((ROW_BLOCK, width), lambda i: (i, 0)),
            pl.BlockSpec(vec.shape, lambda i: (0, 0)),
        ],
        out_specs=[
            pl.BlockSpec((ROW_BLOCK, width), lambda i: (i, 0)),
            pl.BlockSpec((width, ROW_BLOCK), lambda i: (0, i)),
            pl.BlockSpec((1, 128), lambda i: (0, 0)),
        ],
        out_shape=[
            shape((length, width), BF16),
            shape((width, length), BF16),
            shape((1, 128), F32),
        ],
        compiler_params=settings(),
        cost_estimate=cost(0, 10e6),
        name="first_norm",
    )(rows, vec)


def weight_call(kernel, place, weights, grid, in_specs, operands, out_specs, out_shape, name, flops, moved, aliases=None, tile=None):
    arrays = [array for pieces, _ in weights for array, _ in pieces]

    def body(place_ref, *refs):
        at = len(arrays)
        ins = refs[at : at + len(operands)]
        at += len(operands)
        outs = refs[at : at + len(out_shape)]
        at += len(out_shape)
        buffers, sems = refs[at : at + len(weights)], refs[at + len(weights) :]

        copies, ref = [], 0
        for (pieces, _), buffer, sem in zip(weights, buffers, sems):
            first = 0
            for _, plan in pieces:
                copies.append(piece_copies(place_ref, refs[ref], plan, buffer, sem, first))
                ref += 1
                first += len(plan)

        @pl.when(pl.program_id(0) == 0)
        def _():
            for _, group in copies:
                for copy in group:
                    copy.start()
            if tile is None:
                for _, group in copies:
                    for copy in group:
                        copy.wait()

        if tile is not None:
            now = tile(place_ref, pl.program_id(0))
            for at, group in copies:

                @pl.when((pl.program_id(0) == 0) if at is None else (at // TILE == now))
                def _(group=group):
                    for copy in group:
                        copy.wait()

        kernel(place_ref, *ins, *outs, *buffers)

    return pl.pallas_call(
        body,
        grid_spec=pltpu.PrefetchScalarGridSpec(
            num_scalar_prefetch=1,
            grid=grid,
            in_specs=[pl.BlockSpec(memory_space=pltpu.HBM)] * len(arrays) + in_specs,
            out_specs=out_specs,
            scratch_shapes=[pltpu.VMEM((D, columns), BF16) for _, columns in weights]
            + [
                pltpu.SemaphoreType.DMA((sum(len(plan) for _, plan in pieces),))
                for pieces, _ in weights
            ],
        ),
        out_shape=out_shape,
        input_output_aliases={1 + len(arrays) + i: o for i, o in (aliases or {}).items()},
        compiler_params=settings(),
        cost_estimate=cost(flops, moved),
        name=name,
    )(place, *arrays, *operands)


TILE = 1024
GRADIENT_MIB = 57


def whole(array_shape):
    return pl.BlockSpec(array_shape, lambda i, *_: (0,) * len(array_shape))


def row_spec(width, block=ROW_BLOCK):
    return pl.BlockSpec((block, width), lambda i, *_: (i, 0))


def column_spec(height, tile=TILE):
    return pl.BlockSpec((height, tile), lambda i, *_: (0, i))


def tile_of(buffer, index):
    return buffer[:, pl.ds(pl.multiple_of(index * TILE, TILE), TILE)]


def split_spec(height, steps):
    return (
        pl.BlockSpec((height, TILE), lambda i, place: (0, turned_step(place, steps)(i))),
        pl.BlockSpec((height, TILE), lambda i, place: (0, jnp.minimum(i, steps // 2 - 1))),
    )


def project_kernel(place, h_ref, bias_ref, o_ref, buffer):
    o_ref[...] = (mxu(h_ref[...], tile_of(buffer, pl.program_id(0)), NN) + bias_ref[...]).astype(BF16)


def project(normed, bias, weight, place):
    length, width = normed.shape
    columns = bias.shape[1]
    return weight_call(
        project_kernel,
        place,
        [(weight, columns)],
        (columns // TILE,),
        [whole((length, width)), column_spec(1)],
        [normed, bias],
        [column_spec(length)],
        [shape((length, columns), BF16)],
        "project",
        2 * length * width * columns,
        16e6,
        tile=lambda place, i: i,
    )[0]


def join_kernel(place, c_ref, x_ref, vec_ref, middle_ref, h_ref, turned_ref, buffer):
    middle = (
        x_ref[...].astype(F32) + mxu(c_ref[...], buffer[...], NT) + vec_ref[4:5, :]
    )
    middle_ref[...] = middle
    normed = (row_stats(middle)[0] * vec_ref[5:6, :] + vec_ref[6:7, :]).astype(BF16)
    h_ref[...] = normed
    turned_ref[...] = normed.T


def join(context, rows, vec, weight, place):
    length, width = context.shape
    return weight_call(
        join_kernel,
        place,
        [(weight, D)],
        (length // ROW_BLOCK,),
        [row_spec(width), row_spec(D), whole(vec.shape)],
        [context, rows, vec],
        [row_spec(D), row_spec(D), pl.BlockSpec((D, ROW_BLOCK), lambda i, *_: (0, i))],
        [shape((length, D), F32), shape((length, D), BF16), shape((D, length), BF16)],
        "join",
        2 * length * width * D,
        16e6,
    )


def widen_kernel(place, h_ref, bias_ref, a_ref, slope_ref, send_ref, buffer):
    root, cubic = math.sqrt(2.0 / math.pi), 0.044715
    weights = tile_of(buffer, pl.program_id(0))
    for first in range(0, h_ref.shape[0], ROW_BLOCK):
        rows = slice(first, first + ROW_BLOCK)
        u = mxu(h_ref[rows, :], weights, NN) + bias_ref[...]
        square = u * u
        bent = jnp.tanh(u * (root + (root * cubic) * square))
        half = 0.5 * u
        near = 0.5 + 0.5 * bent
        low = (u * near).astype(BF16)
        a_ref[rows, :] = low
        slope_ref[rows, :] = (
            near + half * (1.0 - bent * bent) * (root + (3.0 * root * cubic) * square)
        ).astype(BF16)
        if send_ref is not None:
            send_ref[rows, :] = low


def widen_half(normed, bias, weight, place, before=()):
    length, width = normed.shape
    columns = bias.shape[1]
    steps = columns // TILE // 2

    def at(i, s):
        return (s[3] if before else 1 - s[3]) * steps + i

    full = pl.BlockSpec((length, TILE), lambda i, s: (0, at(i, s)))
    sends = [] if before else [pl.BlockSpec((length, TILE), lambda i, s: (0, i))]

    def kernel(place, h_ref, bias_ref, *refs):
        a_ref, slope_ref, *send, buffer = refs[len(before) :]
        widen_kernel(place, h_ref, bias_ref, a_ref, slope_ref, send[0] if send else None, buffer)

    return weight_call(
        kernel,
        place,
        [(weight, columns // 2)],
        (steps,),
        [whole((length, width)), pl.BlockSpec((1, TILE), lambda i, s: (0, at(i, s)))]
        + [pl.BlockSpec(memory_space=pltpu.HBM)] * len(before),
        [normed, bias, *before],
        [full, full] + sends,
        [shape((length, columns), BF16)] * 2 + [shape((length, columns // 2), BF16)] * len(sends),
        "widen",
        length * width * columns,
        14e6,
        {2: 0, 3: 1} if before else {},
    )


def hidden_back_kernel(steps, place, g_ref, slope_ref, o_ref, send_ref, sum_ref, buffer):
    step = pl.program_id(0)
    weights = tile_of(buffer, turned_step(place, steps)(step))
    total = jnp.zeros((1, TILE), F32)
    for first in range(0, g_ref.shape[0], ROW_BLOCK):
        rows = slice(first, first + ROW_BLOCK)
        grad = (mxu(g_ref[rows, :], weights, NN) * slope_ref[rows, :].astype(F32)).astype(BF16)
        o_ref[rows, :] = grad
        total = total + column_sum(grad.astype(F32))
    sum_ref[pl.ds(turned_step(place, steps)(step), 1), :] = total

    @pl.when(step < steps // 2)
    def _():
        send_ref[...] = o_ref[...]


def hidden_back(cot, slope, weight, place):
    length, width = cot.shape
    columns = slope.shape[1]
    steps = columns // TILE
    full, half = split_spec(length, steps)
    return weight_call(
        partial(hidden_back_kernel, steps),
        place,
        [(weight, columns)],
        (steps,),
        [whole((length, width)), full],
        [cot, slope],
        [full, half, whole((steps, TILE))],
        [
            shape((length, columns), BF16),
            shape((length, columns // 2), BF16),
            shape((steps, TILE), F32),
        ],
        "hidden_back",
        2 * length * width * columns,
        28e6,
        tile=lambda place, i: turned_step(place, steps)(i),
    )


def middle_back_kernel(
    place, gu_ref, x1_ref, g_ref, vec_ref, gx_ref, ga_ref, turned_ref, gc_ref, sums_ref, up, out
):
    upstream = mxu(gu_ref[...], up[...], NT)
    scaled, inverse, _ = row_stats(x1_ref[...])
    grad = g_ref[...].astype(F32) + norm_back(upstream, scaled, inverse, vec_ref[5:6, :])
    gx_ref[...] = grad
    low = grad.astype(BF16)
    ga_ref[...] = low
    turned_ref[...] = low.T
    gc_ref[...] = mxu(low, out[...], NN).astype(BF16)
    accumulate(
        sums_ref,
        jnp.concatenate(
            [
                column_sum(low.astype(F32)),
                column_sum(upstream * scaled),
                column_sum(upstream),
            ],
            axis=0,
        ),
    )


def middle_back(hidden_grad, middle, cot, vec, up, out, place):
    length, columns = hidden_grad.shape
    return weight_call(
        middle_back_kernel,
        place,
        [(up, columns), (out, D)],
        (length // ROW_BLOCK,),
        [row_spec(columns), row_spec(D), row_spec(D), whole(vec.shape)],
        [hidden_grad, middle, cot, vec],
        [
            row_spec(D),
            row_spec(D),
            pl.BlockSpec((D, ROW_BLOCK), lambda i, *_: (0, i)),
            row_spec(D),
            whole((3, D)),
        ],
        [
            shape((length, D), F32),
            shape((length, D), BF16),
            shape((D, length), BF16),
            shape((length, D), BF16),
            shape((3, D), F32),
        ],
        "middle_back",
        2 * length * D * (columns + D),
        36e6,
    )


def input_back_kernel(place, lower_ref, upper_ref, x_ref, gx_ref, vec_ref, o_ref, sums_ref, buffer):
    upstream = None
    for j in range(3):
        for part, ref in enumerate((lower_ref, upper_ref)):
            width = ref.shape[2]
            start = j * D + part * width
            piece = mxu(ref[j], buffer[:, start : start + width], NT)
            upstream = piece if upstream is None else upstream + piece
    scaled, inverse, _ = row_stats(x_ref[...].astype(F32))
    o_ref[...] = gx_ref[...] + norm_back(upstream, scaled, inverse, vec_ref[0:1, :])
    accumulate(
        sums_ref,
        jnp.concatenate([column_sum(upstream * scaled), column_sum(upstream)], axis=0),
    )


def input_back(lower, upper, rows, middle_grad, vec, weight, place):
    length = rows.shape[0]
    half = lower.shape[2]
    stacked = pl.BlockSpec((3, ROW_BLOCK, half), lambda i, *_: (0, i, 0))
    return weight_call(
        input_back_kernel,
        place,
        [(weight, 3 * D)],
        (length // ROW_BLOCK,),
        [stacked, stacked, row_spec(D), row_spec(D), whole(vec.shape)],
        [lower, upper, rows, middle_grad, vec],
        [row_spec(D), whole((2, D))],
        [shape((length, D), F32), shape((2, D), F32)],
        "input_back",
        2 * length * D * 3 * D,
        24e6,
    )


def narrow_kernel(place, a_ref, x1_ref, vec_ref, o_ref, buffer):
    o_ref[...] = x1_ref[...] + mxu(a_ref[...], buffer[...], NT) + vec_ref[11:12, :]


def narrow(active, middle, vec, weight, place, part, before=None):
    length, columns = active.shape
    steps = length // ROW_BLOCK // 2
    others = [] if before is None else [before]

    def rows_of(width):
        return pl.BlockSpec((ROW_BLOCK, width), lambda i, *_: (part * steps + i, 0))

    return weight_call(
        lambda place, a_ref, x1_ref, vec_ref, *refs: narrow_kernel(
            place, a_ref, x1_ref, vec_ref, *refs[-2:]
        ),
        place,
        [(weight, columns)],
        (steps,),
        [rows_of(columns), rows_of(D), whole(vec.shape)]
        + [pl.BlockSpec(memory_space=pltpu.HBM)] * len(others),
        [active, middle, vec, *others],
        [rows_of(D)],
        [shape((length, D), F32)],
        "narrow",
        length * D * columns,
        13e6,
        {3: 0} if others else {},
    )[0]


def gradient_kernel(cut, place, t_ref, t2_ref, r_ref, r2_ref, *refs):
    total = refs[-1]
    total[...] = (
        mxu(t_ref[...], r_ref[0], NN) + mxu(t2_ref[...], r2_ref[0], NN)
    ).astype(BF16)
    step, outs = pl.program_id(0), list(refs[:-1])
    z_count, _, rows, _ = outs[0].shape

    def share(send_ref, keep_ref, x_first):
        for z in range(z_count):
            for other in range(2):
                for ref, away in ((send_ref, True), (keep_ref, False)):
                    x = (1 - place[1] if away else place[1]) if x_first else other
                    y = other if x_first else (1 - place[2] if away else place[2])
                    first = pl.multiple_of(((2 * z + x) * 2 + y) * rows, rows)
                    ref[z, other] = total[pl.ds(first, rows), :]

    if cut:
        send, keep = outs[:2]
        outs = outs[2:]

        @pl.when(step < cut)
        def _():
            share(send, keep, True)

    if outs:

        @pl.when(step >= cut)
        def _():
            share(outs[0], outs[1], False)


def gradient(turned, turned_other, right, right_other, place, n_dp, x_tiles, tiles):
    groups, length, columns = right.shape
    half = columns // 2
    tile = groups * half // tiles
    steps = half // tile
    rows = D // n_dp // 2
    block = (n_dp // 2, 2, rows, tile)
    specs, shapes = [], []
    if x_tiles:
        specs += [pl.BlockSpec(block, lambda i, s: (0, 0, 0, jnp.minimum(i, x_tiles - 1)))] * 2
        shapes += [shape(block[:3] + (x_tiles * tile,), BF16)] * 2
    if x_tiles < tiles:
        specs += [pl.BlockSpec(block, lambda i, s: (0, 0, 0, jnp.maximum(i - x_tiles, 0)))] * 2
        shapes += [shape(block[:3] + ((tiles - x_tiles) * tile,), BF16)] * 2
    fixed = pl.BlockSpec((D, length), lambda i, s: (0, 0))
    return pl.pallas_call(
        partial(gradient_kernel, x_tiles),
        grid_spec=pltpu.PrefetchScalarGridSpec(
            num_scalar_prefetch=1,
            grid=(tiles,),
            in_specs=[
                fixed,
                fixed,
                pl.BlockSpec(
                    (1, length, tile),
                    lambda i, s: (i // steps, 0, s[3] * steps + lax.rem(i, steps)),
                ),
                pl.BlockSpec((1, length, tile), lambda i, s: (i // steps, 0, lax.rem(i, steps))),
            ],
            out_specs=specs,
            scratch_shapes=[pltpu.VMEM((D, tile), BF16)],
        ),
        out_shape=shapes,
        compiler_params=settings(GRADIENT_MIB),
        cost_estimate=cost(4 * D * length * groups * half, 14e6),
        name="gradient",
    )(place, turned, turned_other, right, right_other)


def wide_sum(*terms):
    return reduce(lambda a, b: a + b, [term.astype(F32) for term in terms])


def take(array, index, axis):
    return lax.dynamic_index_in_dim(array, index, axis, keepdims=False)


def near_free():
    return pl.CostEstimate(flops=1, bytes_accessed=1, transcendentals=0)


def assemble(place, arrays, shapes, moves):
    def body(place_ref, *refs):
        sems = refs[-1]
        copies = []
        for n, (source, at, target, to) in enumerate(moves):
            src, dst = refs[source], refs[len(arrays) + target]
            at = at(place_ref) if callable(at) else at
            copies.append(
                pltpu.make_async_copy(
                    src if at is None else src.at[at], dst if to is None else dst.at[to], sems.at[n]
                )
            )
        for copy in copies:
            copy.start()
        for copy in copies:
            copy.wait()

    return pl.pallas_call(
        body,
        grid_spec=pltpu.PrefetchScalarGridSpec(
            num_scalar_prefetch=1,
            grid=(1,),
            in_specs=[pl.BlockSpec(memory_space=pltpu.HBM)] * len(arrays),
            out_specs=[whole(dims) for dims in shapes],
            scratch_shapes=[pltpu.SemaphoreType.DMA((len(moves),))],
        ),
        out_shape=[shape(dims, BF16) for dims in shapes],
        compiler_params=settings(),
        cost_estimate=near_free(),
        name="assemble",
    )(place, *arrays)


def sums_of_two(place, pairs, axes):
    count = len(pairs)

    def body(place_ref, *refs):
        ins, outs = refs[: 2 * count], refs[2 * count : 3 * count]
        buffers, sems = refs[3 * count : 5 * count], refs[-1]
        copies = []
        for n in range(2 * count):
            away = 1 - place_ref[axes[n // 2]]
            copies.append(pltpu.make_async_copy(ins[n].at[:, away], buffers[n], sems.at[n]))
        for copy in copies:
            copy.start()
        for copy in copies:
            copy.wait()
        for n in range(count):
            kept, recv = buffers[2 * n], buffers[2 * n + 1]
            outs[n][...] = (kept[...].astype(F32) + recv[...].astype(F32)).astype(BF16)

    dims = [keep.shape[:1] + keep.shape[2:] for keep, _ in pairs]
    return pl.pallas_call(
        body,
        grid_spec=pltpu.PrefetchScalarGridSpec(
            num_scalar_prefetch=1,
            grid=(1,),
            in_specs=[pl.BlockSpec(memory_space=pltpu.HBM)] * (2 * count),
            out_specs=[whole(d) for d in dims],
            scratch_shapes=[pltpu.VMEM(d, BF16) for d in dims for _ in range(2)]
            + [pltpu.SemaphoreType.DMA((2 * count,))],
        ),
        out_shape=[shape(d, BF16) for d in dims],
        compiler_params=settings(),
        cost_estimate=near_free(),
        name="sums_of_two",
    )(place, *[array for pair in pairs for array in pair])


def sums_of_z(place, terms, axes, picks, recv=None):
    count = len(terms)
    widths = [keep.shape[3] for keep, _, _ in terms]
    rows, total = terms[0][0].shape[2], sum(widths)
    dtypes = [BF16, F32] if recv is not None else [BF16]
    dims = [(rows, total)] * 2 if recv is not None else [(len(picks), rows, total)]
    extra = [] if recv is None else [recv]

    def body(place_ref, *refs):
        ins = refs[: 3 * count]
        add = refs[3 * count : 3 * count + len(extra)]
        at = 3 * count + len(extra)
        outs, buffers, sems = refs[at : at + len(dims)], refs[at + len(dims) : -1], refs[-1]
        copies = []
        for p, (bits, _, _, _) in enumerate(picks):
            z = place_ref[0] ^ bits
            for n in range(3 * count):
                group, part = divmod(n, 3)
                source = ins[n].at[z] if part == 2 else ins[n].at[z, place_ref[axes[group]]]
                copies.append(
                    pltpu.make_async_copy(source, buffers[group].at[p, part], sems.at[len(copies)])
                )
        for copy in copies:
            copy.start()
        for copy in copies:
            copy.wait()
        for p, (_, added, out, row) in enumerate(picks):
            first = 0
            for group, width in enumerate(widths):
                columns = slice(first, first + width)
                first += width
                value = wide_sum(*[buffers[group][p, part] for part in range(3)])
                if added is not None:
                    value = value + add[0][added, :, columns].astype(F32)
                if row is None:
                    outs[out][:, columns] = value.astype(dtypes[out])
                else:
                    outs[out][row, :, columns] = value.astype(dtypes[out])

    return pl.pallas_call(
        body,
        grid_spec=pltpu.PrefetchScalarGridSpec(
            num_scalar_prefetch=1,
            grid=(1,),
            in_specs=[pl.BlockSpec(memory_space=pltpu.HBM)] * (3 * count)
            + [whole(array.shape) for array in extra],
            out_specs=[whole(d) for d in dims],
            scratch_shapes=[pltpu.VMEM((len(picks), 3, rows, width), BF16) for width in widths]
            + [pltpu.SemaphoreType.DMA((len(picks) * 3 * count,))],
        ),
        out_shape=[shape(d, dtype) for d, dtype in zip(dims, dtypes)],
        compiler_params=settings(),
        cost_estimate=near_free(),
        name="sums_of_z",
    )(place, *[array for term in terms for array in term], *extra)


def finish(halves, before=None):
    widths = [total.shape[1] for total, _ in halves]
    rows = halves[0][0].shape[0]
    extra = [] if before is None else [before]

    def body(*refs):
        out, squares = refs[-2:]
        result = refs[2 * len(halves)][...] if extra else jnp.zeros((1, 128), F32)
        first = 0
        for n, width in enumerate(widths):
            value = refs[2 * n][...] + refs[2 * n + 1][...].astype(F32)
            out[:, first : first + width] = value.astype(BF16)
            first += width
            result = result + jnp.sum(value * value)
        squares[...] = result

    return pl.pallas_call(
        body,
        out_shape=[shape((rows, sum(widths)), BF16), shape((1, 128), F32)],
        compiler_params=settings(),
        cost_estimate=near_free(),
        name="finish",
    )(*[array for half in halves for array in half], *extra)


def adam_step(weight, grad, first, second, rate, decay):
    first_next = BETA_ONE * first + (1.0 - BETA_ONE) * grad
    second_next = BETA_TWO * second + (1.0 - BETA_TWO) * grad * grad
    first_hat = first_next / (1.0 - BETA_ONE**STEP)
    second_hat = second_next / (1.0 - BETA_TWO**STEP)
    weight_next = weight - rate * (first_hat / (jnp.sqrt(second_hat) + ADAM_EPS) + decay * weight)
    return (weight_next, first_next, second_next)


def adam_kernel(halves, groups, place, factor, *refs):
    pieces, rest = refs[: 4 * groups], refs[4 * groups :]
    w_ref, m_ref, s_ref, wn_ref, mn_ref, sn_ref, half_ref = rest
    height, width = pieces[0].shape
    step = pl.program_id(0)

    def update(group, core, y, columns):
        choice = (core ^ place[3]) * 2 + (y ^ place[2])
        rows = slice(y * height, (y + 1) * height)
        grad = pieces[4 * group][...]
        for k in (1, 2, 3):
            grad = jnp.where(choice == k, pieces[4 * group + k][...], grad)
        new = adam_step(
            w_ref[rows, columns],
            grad.astype(F32) * factor[0],
            m_ref[rows, columns],
            s_ref[rows, columns],
            MATRIX_RATE,
            DECAY,
        )
        wn_ref[rows, columns], mn_ref[rows, columns], sn_ref[rows, columns] = new
        half_ref[rows, columns] = new[0].astype(BF16)

    for y in range(2):
        if halves == 1:
            update(0, step // 2, y, slice(None))
        else:
            for group in range(groups):

                @pl.when(lax.rem(step, groups) == group)
                def _(group=group):
                    for core in range(2):
                        update(group, core, y, slice(core * width, (core + 1) * width))


def adam(place, factor, pieces, starts, weight, first, second):
    rows, columns = weight.shape
    groups = len(starts)
    if groups == 1:
        steps, tile = 4, columns // 4
        width = tile
        specs = [
            pl.BlockSpec((rows // 2, width), lambda i, *_: (0, starts[0] // width + lax.rem(i, 2)))
        ] * 4
    else:
        steps, tile = columns // 512, 512
        width = tile // 2
        specs = [
            pl.BlockSpec(
                (rows // 2, width), lambda i, *_, start=start: (0, start // width + i // groups)
            )
            for start in starts
            for _ in range(4)
        ]
    block = pl.BlockSpec((rows, tile), lambda i, *_: (0, i))
    full = (rows, columns)
    return pl.pallas_call(
        partial(adam_kernel, tile // width, groups),
        grid_spec=pltpu.PrefetchScalarGridSpec(
            num_scalar_prefetch=2,
            grid=(steps,),
            in_specs=specs + [block] * 3,
            out_specs=[block] * 4,
        ),
        out_shape=[shape(full, F32)] * 3 + [shape(full, BF16)],
        compiler_params=settings(20),
        cost_estimate=cost(0, rows * columns * 28),
        name="adam",
    )(place, factor, *(pieces * groups), weight, first, second)


def tied(values, *others):
    return lax.optimization_barrier((values,) + others)[0]


KERNELS = (
    turn,
    first_norm,
    project,
    attend_forward,
    join,
    widen_half,
    hidden_back,
    middle_back,
    attend_backward,
    gradient,
    input_back,
    narrow,
)


class Order:
    def __init__(self):
        self.last = []
        self.pending = []

    def __call__(self, work, *operands):
        if self.last:
            leaves, tree = jax.tree_util.tree_flatten(operands)
            arrays = [leaf for leaf in leaves if isinstance(leaf, jax.Array)]
            if work in KERNELS:
                arrays[0] = tied(arrays[0], *self.last, *self.pending)
            else:
                arrays = lax.optimization_barrier((*arrays, *self.last, *self.pending))
            arrays = iter(arrays)
            leaves = [next(arrays) if isinstance(leaf, jax.Array) else leaf for leaf in leaves]
            operands = jax.tree_util.tree_unflatten(tree, leaves)
        result = work(*operands)
        self.last, self.pending = jax.tree_util.tree_leaves(result), []
        return result

    def send(self, array, **bits):
        return swap(tied(array, *self.last), **bits)

    def land(self, *arrays):
        self.pending += arrays

    def cross(self, array):
        crossed = swap(tied(array, *self.last, *self.pending), core=1)
        return crossed

    def cross_all(self, *arrays):
        crossed = [self.cross(array) for array in arrays]
        self.pending += crossed
        return crossed


def stack_z(*parts):
    return jnp.stack(parts)


def to_send(own, place, parts, split_y, extra=None):
    mine = pack(own, place, parts, split_y).astype(BF16)
    if extra is None:
        return mine
    flat = extra.astype(BF16).reshape(-1, mine.shape[1])
    spare = -(mine.shape[0] + flat.shape[0]) % 16
    return jnp.concatenate([mine, flat, jnp.zeros((spare, mine.shape[1]), BF16)], axis=0)


def vectors_of(near, far, index, rows, dims, n_dp):
    count = dims[0] * dims[1] // near.shape[2]
    both = jnp.stack([near[:, rows : rows + count], far[:, rows : rows + count]], axis=1)
    both = both.reshape((n_dp,) + dims)
    return jnp.concatenate([take(both, index ^ j, 0) for j in range(n_dp)], axis=1).astype(F32)


def per_device(
    tokens,
    segment_ids,
    cotangent,
    qkv_weight,
    out_weight,
    up_weight,
    down_weight,
    vectors,
    qkv_first,
    qkv_second,
    out_first,
    out_second,
    up_first,
    up_second,
    down_first,
    down_second,
    vectors_first,
    vectors_second,
):
    n_dp, n_rep = lax.axis_size("dp"), lax.axis_size("rep")
    paired = n_dp == 8 and n_rep == 4
    dp, rep = lax.axis_index("dp"), lax.axis_index("rep")
    z, x, y, core = dp // 2, dp % 2, rep // 2, rep % 2
    place = jnp.stack([z, x, y, core]).astype(jnp.int32)
    seq_len = tokens.shape[1]
    segs_column = segment_ids.reshape(seq_len, 1)
    rows = tokens.reshape(seq_len, D)
    cot = cotangent.reshape(seq_len, D)
    up_rows = FF // D
    shard = qkv_weight.shape[0]
    masters = (qkv_weight, out_weight, up_weight, down_weight, vectors)
    pairs = HEADS // 2
    run = Order()

    if paired:

        def held(zs, here, x=0, y=0, there=None):
            return [(here, zs, x, y, 0), (there, zs, x, y, 1)]

        def all_z(mine):
            return [run.send(mine, z=bits) for bits in (1, 2, 3)]

        half, b_two = FF // 2, 3 * D // 4
        straight, zs = (0, 1, 2, 3), (0, 2, 1, 3)
        mine_b = to_send(qkv_weight, place, [(0, D, D // 2)], True, vectors)
        near_b = [swap(mine_b, z=bits) for bits in (1, 2, 3)]
        run.last = [mine_b]
        mine_a = run(to_send, qkv_weight, place, [(2 * D, D // 2, D // 2)], False)
        mine_two = run(
            lambda up, out: jnp.concatenate(
                [
                    pack(up, place, [(D // 2, half, b_two)], True),
                    pack(out, place, [(0, D // 2, D // 2)], False),
                ],
                axis=1,
            ).astype(BF16),
            up_weight,
            out_weight,
        )
        mine_three = run(to_send, down_weight, place, [(0, half, half // 2)], True)
        mine_last = run(to_send, up_weight, place, [(0, half, D // 2)], False)
        stack_b = run(stack_z, mine_b, *near_b)
        far_b, side_b = run.send(stack_b, x=1), run.send(stack_b, y=1)
        near_a = all_z(mine_a)
        cot_turned, down_bias_grad = run(turn, cot)
        run.land(far_b, side_b)
        vec = run(vectors_of, stack_b, far_b, dp, shard, vectors.shape, n_dp)
        across_b = run.send(far_b, y=1)
        stack_a = run(stack_z, mine_a, *near_a)
        far_a, far_two = run.send(stack_a, x=1), run.send(mine_two, z=2)
        near_b_other, far_b_other = run.send(stack_b, core=1), run.send(far_b, core=1)
        normed_one, normed_one_turned, scale_sum = run(first_norm, rows, vec)
        run.land(near_b_other, far_b_other, across_b, far_a, far_two)
        side_b_other, across_b_other, near_a_other, far_a_other = run.cross_all(
            side_b, across_b, stack_a, far_a
        )
        pair_two = run(stack_z, mine_two, far_two)
        other_two = run.send(pair_two, z=1)
        normed_one_turned_other = run.send(normed_one_turned, core=1)
        cot_turned_other = run.send(cot_turned, core=1)
        qkv_all = gathered(
            shard,
            held(straight, stack_b, there=near_b_other)
            + held(straight, far_b, 1, there=far_b_other)
            + held(straight, side_b, 0, 1, side_b_other)
            + held(straight, across_b, 1, 1, across_b_other),
            0,
            D // 2,
            0,
            D,
            D // 2,
        ) + gathered(
            shard,
            held(straight, stack_a, there=near_a_other) + held(straight, far_a, 1, there=far_a_other),
            0,
            D // 2,
            2 * D,
            D // 2,
            0,
        )
    else:
        vec = lax.all_gather(vectors.astype(BF16), "dp", axis=1, tiled=True).astype(F32)
        low = qkv_weight.astype(BF16)
        qkv_all = whole_rows(low)
        out_all, up_all, down_all = (
            whole_rows(own.astype(BF16)) for own in (out_weight, up_weight, down_weight)
        )
        cot_turned, down_bias_grad = run(turn, cot)
        normed_one, normed_one_turned, scale_sum = run(first_norm, rows, vec)

    qkv_bias = jnp.concatenate([vec[2:3], jnp.zeros((1, D), F32), vec[3:4]], axis=1)
    qkv = run(project, normed_one, qkv_bias, qkv_all, place)
    if paired:
        run.land(normed_one_turned_other, cot_turned_other)
        stack_b, stack_a = run(
            lambda *t: assemble(
                place,
                t,
                [(4, shard, b_two), (4, shard, D // 2)],
                [
                    (n, (slice(0, 2), slice(None), columns), out, slice(2 * n, 2 * n + 2))
                    for n in range(2)
                    for out, columns in ((0, slice(0, b_two)), (1, slice(b_two, b_two + D // 2)))
                ],
            ),
            pair_two,
            other_two,
        )
        far_b, side_b = run.send(stack_b, x=1), run.send(stack_b, y=1)
        far_last, far_three = run.send(mine_last, z=2), run.send(mine_three, z=2)
        near_a_other = run.send(stack_a, core=1)
    context, lower_sums = run(attend_forward, qkv, segment_ids, segs_column, 0, pairs // 2)
    if paired:
        run.land(far_b, side_b, near_a_other)
        pair_last, pair_three = run(
            lambda *t: assemble(
                place,
                t,
                [(2, shard, D // 2), (2, shard, half // 2)],
                [(n, None, n // 2, n % 2) for n in range(4)],
            ),
            mine_last,
            far_last,
            mine_three,
            far_three,
        )
        across_b, far_a = run.send(far_b, y=1), run.send(stack_a, x=1)
        other_last, other_three = run.send(pair_last, z=1), run.send(pair_three, z=1)
        near_b_other = run.send(stack_b, core=1)
    context, upper_sums = run(attend_forward, qkv, segment_ids, segs_column, pairs // 2, pairs // 2, context)
    if paired:
        run.land(across_b, far_a, near_b_other, other_last, other_three)
        [far_a_other] = run.cross_all(far_a)

        def other_half(s):
            start = pl.multiple_of((1 - s[3]) * (D // 2), D // 2)
            return (slice(None), pl.ds(start, D // 2))

        stack_last, stack_three, context_send = run(
            lambda *t: assemble(
                place,
                t,
                [(4, shard, D // 2), (4, shard, half // 2), (seq_len, D // 2)],
                [(n, None, n // 2, slice(n % 2 * 2, n % 2 * 2 + 2)) for n in range(4)]
                + [(4, other_half, 2, None)],
            ),
            pair_last,
            other_last,
            pair_three,
            other_three,
            context,
        )
        a_held = held(zs, stack_a, there=near_a_other) + held(zs, far_a, 1, there=far_a_other)
        out_all = gathered(shard, a_held, 0, D // 2, 0, D // 2, 0)
        far_last = run.send(stack_last, x=1)
        side_b_other, far_b_other = run.send(side_b, core=1), run.send(far_b, core=1)
        across_b_other, near_last_other = run.send(across_b, core=1), run.send(stack_last, core=1)
    middle, normed_two, normed_two_turned = run(join, context, rows, vec, out_all, place)
    up_bias = vec[7 : 7 + up_rows].reshape(1, FF)
    if paired:
        run.land(side_b_other, far_b_other, across_b_other, near_last_other, far_last)
        [far_last_other] = run.cross_all(far_last)
        far_three, side_three = run.send(stack_three, x=1), run.send(stack_three, y=1)
        normed_two_turned_other = run.send(normed_two_turned, core=1)
        context_other = run.send(context_send, core=1)
        near_three_other = run.send(stack_three, core=1)
        b_held = (
            held(zs, stack_b, there=near_b_other)
            + held(zs, far_b, 1, there=far_b_other)
            + held(zs, side_b, 0, 1, side_b_other)
            + held(zs, across_b, 1, 1, across_b_other)
        )
        last_held = held(zs, stack_last, there=near_last_other) + held(
            zs, far_last, 1, there=far_last_other
        )
        def up_of(b_held, last_held, core_step):
            return gathered(shard, b_held, 0, b_two, D // 2, core_step, b_two) + gathered(
                shard, last_held, 0, D // 2, 0, core_step, 0
            )

        up_all = up_of(b_held, last_held, half)
        up_there, up_here = (
            up_of([t for t in b_held if t[4] == c], [t for t in last_held if t[4] == c], 0)
            for c in (1, 0)
        )
    else:
        up_there, up_here = (
            [(lax.dynamic_slice_in_dim(up_all[0][0], c * (FF // 2), FF // 2, 1), [up_all[0][1][0][:6] + (FF // 2, 0, 0, 0)])]
            for c in (1 - core, core)
        )
    active, slope, active_send = run(widen_half, normed_two, up_bias, up_there, place)
    if paired:
        run.land(far_three, side_three, normed_two_turned_other, context_other, near_three_other)
        across_three = run.send(far_three, y=1)
        active_other = run.send(active_send, core=1)
        far_three_other, side_three_other = run.send(far_three, core=1), run.send(side_three, core=1)
    active, slope = run(widen_half, normed_two, up_bias, up_here, place, (active, slope))

    if not paired:

        def product(turned, right):
            groups = [
                jnp.dot(turned, right[g], preferred_element_type=F32) for g in range(right.shape[0])
            ]
            return jnp.concatenate(groups, axis=1)

        grad_down = product(cot_turned, active[None])
        hidden_grad, _, up_bias_grad = hidden_back(cot, slope, down_all, place)
        grad_up = product(normed_two_turned, hidden_grad[None])
        middle_grad, branch_grad, branch_turned, context_grad, middle_sums = middle_back(
            hidden_grad, middle, cot, vec, up_all, out_all, place
        )
        grad_out = product(branch_turned, context[None])
        lower, _, lower_bias = attend_backward(
            qkv, segment_ids, segs_column, context_grad, lower_sums, 0, pairs // 2, place
        )
        upper, _, upper_bias = attend_backward(
            qkv, segment_ids, segs_column, context_grad, upper_sums, pairs // 2, pairs // 2, place
        )
        parts = [product(normed_one_turned, grads) for grads in (lower, upper)]
        parts = [[part[:, j * D // 2 : (j + 1) * D // 2] for j in range(3)] for part in parts]
        grad_qkv = jnp.concatenate([t for pair in zip(*parts) for t in pair], axis=1)
    else:


        def cut(turned, right, x_tiles, tiles):
            outs = run(gradient, *turned, *right, place, n_dp, x_tiles, tiles)
            parts = []
            if x_tiles:
                parts.append((outs[1], run.send(outs[0], x=1), 2, {"y": 1}))
            if x_tiles < tiles:
                parts.append((outs[-1], run.send(outs[-2], y=1), 1, {"x": 1}))
            return parts

        def cut_again(parts):
            sends = run(
                lambda pairs: sums_of_two(place, pairs, [part[2] for part in parts]),
                [part[:2] for part in parts],
            )
            return [
                (keep, recv, run.send(send, **way), axis)
                for (keep, recv, axis, way), send in zip(parts, sends)
            ]

        def along_z(terms):
            axes = [term[3] for term in terms]
            [send] = run(
                lambda t: sums_of_z(place, t, axes, [(1, None, 0, 0), (3, None, 0, 1)]),
                [term[:3] for term in terms],
            )
            return terms, run.send(send, z=1)

        def along_z_again(terms, recv):
            axes = [term[3] for term in terms]
            send, total = run(
                lambda t, r: sums_of_z(place, t, axes, [(2, 1, 0, None), (0, 0, 1, None)], r),
                [term[:3] for term in terms],
                recv,
            )
            return total, run.send(send, z=2)

        run.land(active_other, far_three_other, side_three_other)
        cut_down = cut((cot_turned, cot_turned_other), (active[None], active_other[None]), 2, 4)
        run.land(across_three)
        [across_three_other] = run.cross_all(across_three)
        down_all = gathered(
            shard,
            held(zs, stack_three, there=near_three_other)
            + held(zs, far_three, 1, there=far_three_other)
            + held(zs, side_three, 0, 1, side_three_other)
            + held(zs, across_three, 1, 1, across_three_other),
            0,
            FF // 4,
            0,
            half,
            FF // 4,
        )
        hidden_grad, hidden_send, up_bias_grad = run(hidden_back, cot, slope, down_all, place)
        terms_down = cut_again(cut_down)
        hidden_other = run.send(hidden_send, core=1)
        middle_grad, branch_grad, branch_turned, context_grad, middle_sums = run(
            middle_back, hidden_grad, middle, cot, vec, up_all, out_all, place
        )
        run.land(hidden_other)
        z_down = along_z(terms_down)
        branch_turned_other = run.send(branch_turned, core=1)
        cut_up = cut(
            (normed_two_turned, normed_two_turned_other), (hidden_grad[None], hidden_other[None]), 2, 4
        )
        run.land(branch_turned_other)
        half_down = along_z_again(*z_down)
        lower, lower_send, lower_bias = run(
            attend_backward, qkv, segment_ids, segs_column, context_grad, lower_sums, 0, pairs // 2, place
        )
        run.land(half_down[1])
        terms_up = cut_again(cut_up)
        lower_other = run.send(lower_send, core=1)
        cut_out = cut((branch_turned, branch_turned_other), (context[None], context_other[None]), 0, 1)
        run.land(lower_other)
        upper, upper_send, upper_bias = run(
            attend_backward,
            qkv,
            segment_ids,
            segs_column,
            context_grad,
            upper_sums,
            pairs // 2,
            pairs // 2,
            place,
        )
        terms_out = cut_again(cut_out)
        upper_other = run.send(upper_send, core=1)
        turned_pair = (normed_one_turned, normed_one_turned_other)
        cut_lower = cut(turned_pair, (lower, lower_other), 1, 3)
        run.land(terms_out[0][2], upper_other)
        cut_upper = cut(turned_pair, (upper, upper_other), 2, 3)
        z_up = along_z(terms_up)
    input_grad, input_sums = run(
        input_back, lower, upper, rows, middle_grad, vec, qkv_all, place
    )
    grad_vec = jnp.concatenate(
        [
            input_sums,
            jnp.concatenate([lower_bias, upper_bias], axis=1),
            middle_sums,
            up_bias_grad.reshape(up_rows, D),
            down_bias_grad,
            jnp.broadcast_to(scale_sum[:, :1], (1, D)),
        ],
        axis=0,
    )
    if paired:
        run.land(*[part[1] for part in cut_lower + cut_upper])
        [vec_recv] = run.cross_all(grad_vec)
        grad_vec = grad_vec + vec_recv
        terms_last = cut_again(cut_lower + cut_upper)
        half_up = along_z_again(*z_up)
    block_out = run(narrow, active, middle, vec, down_all, place, 0)
    if paired:
        z_late = along_z(terms_out + terms_last)
        early, squares = run(finish, [half_down, half_up])
        early_other = run.send(early, y=1)
        vec_recv = run.send(grad_vec, y=1)
    block_out = run(narrow, active, middle, vec, down_all, place, 1, block_out)
    if paired:
        half_late = along_z_again(*z_late)
        for bits in ({"x": 1}, {"z": 1}):
            grad_vec = run(lambda a, b: a + b, grad_vec, vec_recv)
            vec_recv = run.send(grad_vec, **bits)
        grad_vec = run(lambda a, b: a + b, grad_vec, vec_recv)
        vec_recv = run.send(grad_vec, z=2)
    total_rows = seq_len * n_dp * n_rep
    firsts = (qkv_first, out_first, up_first, down_first)
    seconds = (qkv_second, out_second, up_second, down_second)
    if paired:
        late, squares = run(finish, [half_late], squares)
        squares = squares + swap(squares, core=1)
        squares = squares + swap(squares, y=1)
        late_other = swap(tied(late, squares), y=1)
        for bits in ({"x": 1}, {"z": 1}, {"z": 2}):
            squares = squares + swap(squares, **bits)
        squares = squares[0, 0]
        grad_vec = grad_vec + vec_recv
    else:
        shards = [
            lax.psum(lax.psum_scatter(grad, "dp", scatter_dimension=0, tiled=True), "rep")
            for grad in (grad_qkv, grad_out, grad_up, grad_down)
        ]
        grad_vec = lax.psum(grad_vec, AXES)
        squares = lax.psum(reduce(lambda a, b: a + b, [jnp.sum(p * p) for p in shards]), "dp")
    input_scale = grad_vec[12, 0] / total_rows
    grad_vec = grad_vec[:12]
    grad_norm = jnp.sqrt(squares + jnp.sum(grad_vec * grad_vec))
    clip_factor = jnp.minimum(1.0, CLIP_NORM / (grad_norm + 1e-06))
    updates = []
    if paired:
        early = [early, early_other, swap(early, core=1), swap(early_other, core=1)]
        late = [late, late_other, swap(late, core=1), swap(late_other, core=1)]
        factor = clip_factor.reshape(1)
        sources = [
            (late, [D // 2, D // 2 + 3 * D // 4]),
            (late, [0]),
            (early, [half]),
            (early, [0]),
        ]
        for (pieces, starts), weight, first, second in zip(sources, masters, firsts, seconds):
            updates.append(adam(place, factor, pieces, starts, weight, first, second))
    else:
        for grad, weight, first, second in zip(shards, masters, firsts, seconds):
            new = adam_step(weight, grad * clip_factor, first, second, MATRIX_RATE, DECAY)
            updates.append(new + (new[0].astype(BF16),))
    width = vectors.shape[1]
    vec_shard = lax.dynamic_slice_in_dim(grad_vec, dp * width, width, 1)
    new = adam_step(
        vectors, vec_shard * clip_factor, vectors_first, vectors_second, VECTOR_RATE, 0.0
    )
    updates.append(new + (new[0].astype(BF16),))
    return (
        (
            block_out.reshape(1, seq_len, D),
            input_grad.reshape(1, seq_len, D),
            grad_norm,
            input_scale,
        )
        + tuple(update[0] for update in updates)
        + tuple(update[1] for update in updates)
        + tuple(update[2] for update in updates)
        + tuple(update[3] for update in updates)
    )


def solution(mesh):
    rows = P(("dp", "rep"), None, None)
    matrix, vector = P("dp", None), P(None, "dp")
    weights = (matrix,) * 4 + (vector,)
    return jax.shard_map(
        per_device,
        mesh=mesh,
        in_specs=(rows, P(("dp", "rep"), None), rows)
        + weights
        + (matrix,) * 8
        + (vector,) * 2,
        out_specs=(rows, rows, P(), P()) + weights * 4,
        check_vma=False,
    )
```

```python
from functools import partial
from functools import reduce
import math

import jax
import jax.numpy as jnp
from jax import lax
from jax.experimental import pallas as pl
from jax.experimental.pallas import tpu as pltpu
from jax.sharding import PartitionSpec as P

HEADS = 16
HEAD_DIM = 64
D = 1024
FF = 4096
STEP = 10


LN_EPS = 1e-05
CLIP_NORM = 1.0
BETA_ONE = 0.9
BETA_TWO = 0.95
ADAM_EPS = 1e-08
MATRIX_RATE = 0.1
VECTOR_RATE = 1.0
DECAY = 0.1
MASKED = -1e30

F32 = jnp.float32
BF16 = jnp.bfloat16
AXES = ("dp", "rep")
MIB = 2**20
NN = (((1,), (0,)), ((), ()))
NT = (((1,), (1,)), ((), ()))
TN = (((0,), (0,)), ((), ()))


def mxu(left, right, dims):
    return lax.dot_general(left, right, dims, preferred_element_type=F32)


def shape(dims, dtype):
    return jax.ShapeDtypeStruct(dims, dtype)


def settings(mib=56):
    return pltpu.CompilerParams(vmem_limit_bytes=mib * MIB)


SCALE = 50


def cost(flops, moved):
    return pl.CostEstimate(flops=int(SCALE * flops), bytes_accessed=int(SCALE * moved), transcendentals=0)


def swap(values, z=0, x=0, y=0, core=0):
    n_dp, n_rep = lax.axis_size("dp"), lax.axis_size("rep")
    dp_bits, rep_bits = 2 * z + x, 2 * y + core
    pairs = [
        (dp * n_rep + rep, (dp ^ dp_bits) * n_rep + (rep ^ rep_bits))
        for dp in range(n_dp)
        for rep in range(n_rep)
    ]
    return lax.ppermute(values, AXES, pairs)


def pack(own, place, parts, split_y):
    mine = []
    for low, core_step, width in parts:
        start = low + place[3] * core_step + (place[2] * width if split_y else 0)
        mine.append(lax.dynamic_slice_in_dim(own, start, width, 1))
    return mine[0] if len(mine) == 1 else jnp.concatenate(mine, axis=1)


def gathered(rows, stacks, column, width, target, half, y_step):
    return [
        (array, [(z, x, y, core, rows, column, width, target, half, y_step) for z in zs])
        for array, zs, x, y, core in stacks
    ]


def whole_rows(own):
    full = lax.all_gather(own, "dp", axis=0, tiled=True)
    return [(full, [(0, 0, 0, 0, full.shape[0], 0, full.shape[1], 0, 0, 0)])]


def piece_copies(place, ref, plan, target, sems, first):
    copies, at = [], None
    for i, (z, x, y, core, rows, column, width, start, half, y_step) in enumerate(plan):
        if len(ref.shape) == 3:
            row = pl.multiple_of(((place[0] ^ z) * 2 + (place[1] ^ x)) * rows, rows)
            at = start + (place[3] ^ core) * half + (place[2] ^ y) * y_step
            column_at = pl.multiple_of(at, 128)
            source = ref.at[i, pl.ds(0, rows), pl.ds(column, width)]
        else:
            row, column_at, source = 0, start, ref
        copies.append(
            pltpu.make_async_copy(
                source, target.at[pl.ds(row, rows), pl.ds(column_at, width)], sems.at[first + i]
            )
        )
    return at, copies


def turned_step(place, steps):
    half = steps // 2
    return lambda i, *_: lax.rem((1 - place[3]) * half + i, steps)


QUERY_BLOCK = 128
KEY_SPAN = 512


def bands(length):
    return [
        (b * QUERY_BLOCK, max(0, b * QUERY_BLOCK - KEY_SPAN), (b + 1) * QUERY_BLOCK)
        for b in range(length // QUERY_BLOCK)
    ]


def head_slope(head):
    return jnp.exp2(-8.0 * (head.astype(F32) + 1.0) / HEADS)


def head_lanes(h):
    lane = lax.broadcasted_iota(jnp.int32, (1, 2 * HEAD_DIM), 1)
    return (lane >= HEAD_DIM) if h else (lane < HEAD_DIM)


def both_heads(rows):
    return jnp.concatenate([jnp.where(head_lanes(h), rows, BF16(0)) for h in range(2)], axis=0)


def own_lanes(rows):
    half = rows.shape[0] // 2
    return jnp.where(head_lanes(0), rows[:half], rows[half:])


def fill_base(segs_row, segs_column, base, length):
    for b, (first, low, high) in enumerate(bands(length)):
        keys = low + lax.broadcasted_iota(jnp.int32, (high - low, QUERY_BLOCK), 0)
        rows = first + lax.broadcasted_iota(jnp.int32, (high - low, QUERY_BLOCK), 1)
        allowed = (keys <= rows) & (
            segs_column[low:high, :] == segs_row[:, first : first + QUERY_BLOCK]
        )
        base[b, : high - low, :] = jnp.where(allowed, (keys - rows).astype(F32), MASKED)


def biased(scores, base, pair):
    return jnp.concatenate(
        [
            scores[:, h * QUERY_BLOCK : (h + 1) * QUERY_BLOCK] + head_slope(2 * pair + h) * base
            for h in range(2)
        ],
        axis=1,
    )


def attend_forward_kernel(
    first_pair, segs_row, segs_column, q_ref, k_ref, v_ref, *refs
):
    c_ref, lse_ref, base = refs[-3:]
    length = q_ref.shape[0]

    @pl.when(pl.program_id(0) == 0)
    def _():
        fill_base(segs_row, segs_column, base, length)

    pair = first_pair + pl.program_id(0)
    for b, (first, low, high) in enumerate(bands(length)):
        rows = slice(first, first + QUERY_BLOCK)
        queries, keys, values = q_ref[rows, :], k_ref[low:high, :], v_ref[low:high, :]
        scaled = both_heads(queries * BF16(1.0 / math.sqrt(HEAD_DIM)))
        scores = biased(mxu(keys, scaled, NT), base[b, : high - low, :], pair)
        top = jnp.max(scores, axis=0, keepdims=True)
        weights = jnp.exp(scores - top)
        total = jnp.sum(weights, axis=0, keepdims=True)
        probs = (weights * (1.0 / total)).astype(BF16)
        c_ref[rows, :] = own_lanes(mxu(probs, values, TN)).astype(BF16)
        lse = top + jnp.log(total)
        for h in range(2):
            lse_ref[0, h : h + 1, rows] = lse[:, h * QUERY_BLOCK : (h + 1) * QUERY_BLOCK]


def attend_forward(qkv, segs, segs_column, first_pair, pairs, context=None):
    length, width = qkv.shape[0], 2 * HEAD_DIM
    per = D // width
    before = [] if context is None else [context]
    return pl.pallas_call(
        partial(attend_forward_kernel, first_pair),
        grid=(pairs,),
        in_specs=[
            pl.BlockSpec((1, length), lambda i: (0, 0)),
            pl.BlockSpec((length, 1), lambda i: (0, 0)),
            pl.BlockSpec((length, width), lambda i: (0, first_pair + i)),
            pl.BlockSpec((length, width), lambda i: (0, per + first_pair + i)),
            pl.BlockSpec((length, width), lambda i: (0, 2 * per + first_pair + i)),
        ]
        + [pl.BlockSpec(memory_space=pltpu.HBM)] * len(before),
        out_specs=[
            pl.BlockSpec((length, width), lambda i: (0, first_pair + i)),
            pl.BlockSpec((1, 2, length), lambda i: (i, 0, 0)),
        ],
        input_output_aliases={5: 0} if before else {},
        out_shape=[
            shape((length, D), BF16),
            shape((pairs, 2, length), F32),
        ],
        scratch_shapes=[pltpu.VMEM((length // QUERY_BLOCK, KEY_SPAN + QUERY_BLOCK, QUERY_BLOCK), F32)],
        compiler_params=settings(),
        cost_estimate=cost(3.5e9 * pairs, 1e6 * pairs),
        name="attend_forward",
    )(segs, segs_column, qkv, qkv, qkv, *before)


def attend_backward_kernel(
    first_pair,
    pairs,
    place,
    segs_row,
    segs_column,
    q_ref,
    k_ref,
    v_ref,
    g_ref,
    lse_ref,
    o_ref,
    send_ref,
    sums_ref,
    base,
    dk,
    dv,
):
    length = q_ref.shape[0]

    @pl.when(pl.program_id(0) == 0)
    def _():
        fill_base(segs_row, segs_column, base, length)

    pair = first_pair + turned_step(place, pairs)(pl.program_id(0))
    dk[...] = jnp.zeros_like(dk)
    dv[...] = jnp.zeros_like(dv)
    query_sum = jnp.zeros((1, 2 * HEAD_DIM), F32)
    inv_root = BF16(1.0 / math.sqrt(HEAD_DIM))
    for b, (first, low, high) in enumerate(bands(length)):
        rows = slice(first, first + QUERY_BLOCK)
        keys, values = k_ref[low:high, :], v_ref[low:high, :]
        queries, grads = both_heads(q_ref[rows, :]), both_heads(g_ref[rows, :])
        scores = biased(mxu(keys, queries * inv_root, NT), base[b, : high - low, :], pair)
        lse = jnp.concatenate([lse_ref[0, h : h + 1, rows] for h in range(2)], axis=1)
        probs = jnp.exp(scores - lse)
        prob_grad = mxu(values, grads * inv_root, NT)
        row_dot = jnp.sum(probs * prob_grad, axis=0, keepdims=True)
        score_grad = (probs * (prob_grad - row_dot)).astype(BF16)
        dv[low:high, :] += mxu(probs.astype(BF16), grads, NN)
        dk[low:high, :] += mxu(score_grad, queries, NN)
        dq = own_lanes(mxu(score_grad, keys, TN)).astype(BF16)
        o_ref[0, rows, :] = dq
        query_sum = query_sum + jnp.sum(dq.astype(F32), axis=0, keepdims=True)
    o_ref[1] = dk[...].astype(BF16)
    value_grad = dv[...].astype(BF16)
    o_ref[2] = value_grad
    sums_ref[0:1, :] = query_sum
    sums_ref[1:2, :] = jnp.sum(value_grad.astype(F32), axis=0, keepdims=True)

    @pl.when(pl.program_id(0) < pairs // 2)
    def _():
        send_ref[...] = o_ref[...]


def attend_backward(qkv, segs, segs_column, grads, lse, first_pair, pairs, place):
    length, width = qkv.shape[0], 2 * HEAD_DIM
    per = D // width

    def heads(first):
        return pl.BlockSpec(
            (length, width), lambda i, s: (0, first + first_pair + turned_step(s, pairs)(i))
        )

    return pl.pallas_call(
        partial(attend_backward_kernel, first_pair, pairs),
        grid_spec=pltpu.PrefetchScalarGridSpec(
            num_scalar_prefetch=1,
            grid=(pairs,),
            in_specs=[
                pl.BlockSpec((1, length), lambda i, s: (0, 0)),
                pl.BlockSpec((length, 1), lambda i, s: (0, 0)),
                heads(0),
                heads(per),
                heads(2 * per),
                heads(0),
                pl.BlockSpec((1, 2, length), lambda i, s: (turned_step(s, pairs)(i), 0, 0)),
            ],
            out_specs=[
                pl.BlockSpec((3, length, width), lambda i, s: (0, 0, turned_step(s, pairs)(i))),
                pl.BlockSpec((3, length, width), lambda i, s: (0, 0, jnp.minimum(i, pairs // 2 - 1))),
                pl.BlockSpec((2, width), lambda i, s: (0, turned_step(s, pairs)(i))),
            ],
            scratch_shapes=[
                pltpu.VMEM((length // QUERY_BLOCK, KEY_SPAN + QUERY_BLOCK, QUERY_BLOCK), F32),
                pltpu.VMEM((length, width), F32),
                pltpu.VMEM((length, width), F32),
            ],
        ),
        out_shape=[
            shape((3, length, pairs * width), BF16),
            shape((3, length, pairs * width // 2), BF16),
            shape((2, pairs * width), F32),
        ],
        compiler_params=settings(),
        cost_estimate=cost(5e9 * pairs, 1e6 * pairs),
        name="attend_backward",
    )(place, segs, segs_column, qkv, qkv, qkv, grads, lse)


ROW_BLOCK = 256
EARLY_BLOCK = 512


def row_stats(values):
    centre = jnp.mean(values, axis=-1, keepdims=True)
    shifted = values - centre
    spread = jnp.mean(shifted * shifted, axis=-1, keepdims=True)
    inverse = lax.rsqrt(spread + LN_EPS)
    return shifted * inverse, inverse, spread


def norm_back(upstream, scaled, inverse, gain_row):
    weighted = upstream * gain_row
    return inverse * (
        weighted
        - jnp.mean(weighted, axis=-1, keepdims=True)
        - scaled * jnp.mean(weighted * scaled, axis=-1, keepdims=True)
    )


def column_sum(values):
    return jnp.sum(values, axis=0, keepdims=True)


def accumulate(ref, values):
    step = pl.program_id(0)

    @pl.when(step == 0)
    def _():
        ref[...] = values

    @pl.when(step > 0)
    def _():
        ref[...] += values


def turn_kernel(g_ref, turned_ref, sum_ref):
    values = g_ref[...]
    turned_ref[...] = values.T
    accumulate(sum_ref, column_sum(values.astype(F32)))


def turn(cot):
    length, width = cot.shape
    return pl.pallas_call(
        turn_kernel,
        grid=(length // EARLY_BLOCK,),
        in_specs=[pl.BlockSpec((EARLY_BLOCK, width), lambda i: (i, 0))],
        out_specs=[
            pl.BlockSpec((width, EARLY_BLOCK), lambda i: (0, i)),
            pl.BlockSpec((1, width), lambda i: (0, 0)),
        ],
        out_shape=[shape((width, length), BF16), shape((1, width), F32)],
        compiler_params=settings(),
        cost_estimate=cost(0, 8e6),
        name="turn",
    )(cot)


def first_norm_kernel(x_ref, vec_ref, h_ref, turned_ref, scale_ref):
    scaled, _, spread = row_stats(x_ref[...].astype(F32))
    normed = (scaled * vec_ref[0:1, :] + vec_ref[1:2, :]).astype(BF16)
    h_ref[...] = normed
    turned_ref[...] = normed.T
    accumulate(scale_ref, jnp.broadcast_to(column_sum(jnp.sqrt(spread + LN_EPS)), (1, 128)))


def first_norm(rows, vec):
    length, width = rows.shape
    return pl.pallas_call(
        first_norm_kernel,
        grid=(length // EARLY_BLOCK,),
        in_specs=[
            pl.BlockSpec((EARLY_BLOCK, width), lambda i: (i, 0)),
            pl.BlockSpec(vec.shape, lambda i: (0, 0)),
        ],
        out_specs=[
            pl.BlockSpec((EARLY_BLOCK, width), lambda i: (i, 0)),
            pl.BlockSpec((width, EARLY_BLOCK), lambda i: (0, i)),
            pl.BlockSpec((1, 128), lambda i: (0, 0)),
        ],
        out_shape=[
            shape((length, width), BF16),
            shape((width, length), BF16),
            shape((1, 128), F32),
        ],
        compiler_params=settings(),
        cost_estimate=cost(0, 10e6),
        name="first_norm",
    )(rows, vec)


def weight_call(kernel, place, weights, grid, in_specs, operands, out_specs, out_shape, name, flops, moved, aliases=None, tile=None):
    arrays = [array for pieces, _ in weights for array, _ in pieces]

    def body(place_ref, *refs):
        at = len(arrays)
        ins = refs[at : at + len(operands)]
        at += len(operands)
        outs = refs[at : at + len(out_shape)]
        at += len(out_shape)
        buffers, sems = refs[at : at + len(weights)], refs[at + len(weights) :]

        copies, ref = [], 0
        for (pieces, _), buffer, sem in zip(weights, buffers, sems):
            first = 0
            for _, plan in pieces:
                copies.append(piece_copies(place_ref, refs[ref], plan, buffer, sem, first))
                ref += 1
                first += len(plan)

        @pl.when(pl.program_id(0) == 0)
        def _():
            for _, group in copies:
                for copy in group:
                    copy.start()
            if tile is None:
                for _, group in copies:
                    for copy in group:
                        copy.wait()

        if tile is not None:
            now = tile(place_ref, pl.program_id(0))
            for at, group in copies:

                @pl.when((pl.program_id(0) == 0) if at is None else (at // TILE == now))
                def _(group=group):
                    for copy in group:
                        copy.wait()

        kernel(place_ref, *ins, *outs, *buffers)

    return pl.pallas_call(
        body,
        grid_spec=pltpu.PrefetchScalarGridSpec(
            num_scalar_prefetch=1,
            grid=grid,
            in_specs=[pl.BlockSpec(memory_space=pltpu.HBM)] * len(arrays) + in_specs,
            out_specs=out_specs,
            scratch_shapes=[pltpu.VMEM((D, columns), BF16) for _, columns in weights]
            + [
                pltpu.SemaphoreType.DMA((sum(len(plan) for _, plan in pieces),))
                for pieces, _ in weights
            ],
        ),
        out_shape=out_shape,
        input_output_aliases={1 + len(arrays) + i: o for i, o in (aliases or {}).items()},
        compiler_params=settings(),
        cost_estimate=cost(flops, moved),
        name=name,
    )(place, *arrays, *operands)


TILE = 1024
GRADIENT_MIB = 57


def whole(array_shape):
    return pl.BlockSpec(array_shape, lambda i, *_: (0,) * len(array_shape))


def row_spec(width, block=ROW_BLOCK):
    return pl.BlockSpec((block, width), lambda i, *_: (i, 0))


def column_spec(height, tile=TILE):
    return pl.BlockSpec((height, tile), lambda i, *_: (0, i))


def tile_of(buffer, index):
    return buffer[:, pl.ds(pl.multiple_of(index * TILE, TILE), TILE)]


def split_spec(height, steps):
    return (
        pl.BlockSpec((height, TILE), lambda i, place: (0, turned_step(place, steps)(i))),
        pl.BlockSpec((height, TILE), lambda i, place: (0, jnp.minimum(i, steps // 2 - 1))),
    )


def project_kernel(place, h_ref, bias_ref, o_ref, buffer):
    o_ref[...] = (mxu(h_ref[...], tile_of(buffer, pl.program_id(0)), NN) + bias_ref[...]).astype(BF16)


def project(normed, bias, weight, place):
    length, width = normed.shape
    columns = bias.shape[1]
    return weight_call(
        project_kernel,
        place,
        [(weight, columns)],
        (columns // TILE,),
        [whole((length, width)), column_spec(1)],
        [normed, bias],
        [column_spec(length)],
        [shape((length, columns), BF16)],
        "project",
        2 * length * width * columns,
        16e6,
        tile=lambda place, i: i,
    )[0]


def join_kernel(place, c_ref, x_ref, vec_ref, middle_ref, h_ref, turned_ref, buffer):
    middle = (
        x_ref[...].astype(F32) + mxu(c_ref[...], buffer[...], NT) + vec_ref[4:5, :]
    )
    middle_ref[...] = middle
    normed = (row_stats(middle)[0] * vec_ref[5:6, :] + vec_ref[6:7, :]).astype(BF16)
    h_ref[...] = normed
    turned_ref[...] = normed.T


def join(context, rows, vec, weight, place):
    length, width = context.shape
    return weight_call(
        join_kernel,
        place,
        [(weight, D)],
        (length // ROW_BLOCK,),
        [row_spec(width), row_spec(D), whole(vec.shape)],
        [context, rows, vec],
        [row_spec(D), row_spec(D), pl.BlockSpec((D, ROW_BLOCK), lambda i, *_: (0, i))],
        [shape((length, D), F32), shape((length, D), BF16), shape((D, length), BF16)],
        "join",
        2 * length * width * D,
        16e6,
    )


def widen_kernel(place, h_ref, bias_ref, a_ref, slope_ref, send_ref, buffer):
    root, cubic = math.sqrt(2.0 / math.pi), 0.044715
    weights = tile_of(buffer, pl.program_id(0))
    for first in range(0, h_ref.shape[0], ROW_BLOCK):
        rows = slice(first, first + ROW_BLOCK)
        u = mxu(h_ref[rows, :], weights, NN) + bias_ref[...]
        square = u * u
        bent = jnp.tanh(u * (root + (root * cubic) * square))
        near = 0.5 + 0.5 * bent
        full = u * near
        low = full.astype(BF16)
        a_ref[rows, :] = low
        slope_ref[rows, :] = (
            near + full * (1.0 - near) * (2.0 * root + (6.0 * root * cubic) * square)
        ).astype(BF16)
        if send_ref is not None:
            send_ref[rows, :] = low


def widen_half(normed, bias, weight, place, before=()):
    length, width = normed.shape
    columns = bias.shape[1]
    steps = columns // TILE // 2

    def at(i, s):
        return (s[3] if before else 1 - s[3]) * steps + i

    full = pl.BlockSpec((length, TILE), lambda i, s: (0, at(i, s)))
    sends = [] if before else [pl.BlockSpec((length, TILE), lambda i, s: (0, i))]

    def kernel(place, h_ref, bias_ref, *refs):
        a_ref, slope_ref, *send, buffer = refs[len(before) :]
        widen_kernel(place, h_ref, bias_ref, a_ref, slope_ref, send[0] if send else None, buffer)

    return weight_call(
        kernel,
        place,
        [(weight, columns // 2)],
        (steps,),
        [whole((length, width)), pl.BlockSpec((1, TILE), lambda i, s: (0, at(i, s)))]
        + [pl.BlockSpec(memory_space=pltpu.HBM)] * len(before),
        [normed, bias, *before],
        [full, full] + sends,
        [shape((length, columns), BF16)] * 2 + [shape((length, columns // 2), BF16)] * len(sends),
        "widen",
        length * width * columns,
        14e6,
        {2: 0, 3: 1} if before else {},
    )


def hidden_back_kernel(steps, place, g_ref, slope_ref, o_ref, send_ref, sum_ref, buffer):
    step = pl.program_id(0)
    weights = tile_of(buffer, turned_step(place, steps)(step))
    total = jnp.zeros((1, TILE), F32)
    for first in range(0, g_ref.shape[0], ROW_BLOCK):
        rows = slice(first, first + ROW_BLOCK)
        grad = (mxu(g_ref[rows, :], weights, NN) * slope_ref[rows, :].astype(F32)).astype(BF16)
        o_ref[rows, :] = grad
        total = total + column_sum(grad.astype(F32))
    sum_ref[pl.ds(turned_step(place, steps)(step), 1), :] = total

    @pl.when(step < steps // 2)
    def _():
        send_ref[...] = o_ref[...]


def hidden_back(cot, slope, weight, place):
    length, width = cot.shape
    columns = slope.shape[1]
    steps = columns // TILE
    full, half = split_spec(length, steps)
    return weight_call(
        partial(hidden_back_kernel, steps),
        place,
        [(weight, columns)],
        (steps,),
        [whole((length, width)), full],
        [cot, slope],
        [full, half, whole((steps, TILE))],
        [
            shape((length, columns), BF16),
            shape((length, columns // 2), BF16),
            shape((steps, TILE), F32),
        ],
        "hidden_back",
        2 * length * width * columns,
        28e6,
        tile=lambda place, i: turned_step(place, steps)(i),
    )


def middle_back_kernel(
    place, gu_ref, x1_ref, g_ref, vec_ref, gx_ref, ga_ref, turned_ref, gc_ref, sums_ref, up, out
):
    upstream = mxu(gu_ref[...], up[...], NT)
    scaled, inverse, _ = row_stats(x1_ref[...])
    grad = g_ref[...].astype(F32) + norm_back(upstream, scaled, inverse, vec_ref[5:6, :])
    gx_ref[...] = grad
    low = grad.astype(BF16)
    ga_ref[...] = low
    turned_ref[...] = low.T
    gc_ref[...] = mxu(low, out[...], NN).astype(BF16)
    accumulate(
        sums_ref,
        jnp.concatenate(
            [
                column_sum(low.astype(F32)),
                column_sum(upstream * scaled),
                column_sum(upstream),
            ],
            axis=0,
        ),
    )


def middle_back(hidden_grad, middle, cot, vec, up, out, place):
    length, columns = hidden_grad.shape
    return weight_call(
        middle_back_kernel,
        place,
        [(up, columns), (out, D)],
        (length // ROW_BLOCK,),
        [row_spec(columns), row_spec(D), row_spec(D), whole(vec.shape)],
        [hidden_grad, middle, cot, vec],
        [
            row_spec(D),
            row_spec(D),
            pl.BlockSpec((D, ROW_BLOCK), lambda i, *_: (0, i)),
            row_spec(D),
            whole((3, D)),
        ],
        [
            shape((length, D), F32),
            shape((length, D), BF16),
            shape((D, length), BF16),
            shape((length, D), BF16),
            shape((3, D), F32),
        ],
        "middle_back",
        2 * length * D * (columns + D),
        36e6,
    )


def input_back_kernel(place, lower_ref, upper_ref, x_ref, gx_ref, vec_ref, o_ref, sums_ref, buffer):
    upstream = None
    for j in range(3):
        for part, ref in enumerate((lower_ref, upper_ref)):
            width = ref.shape[2]
            start = j * D + part * width
            piece = mxu(ref[j], buffer[:, start : start + width], NT)
            upstream = piece if upstream is None else upstream + piece
    scaled, inverse, _ = row_stats(x_ref[...].astype(F32))
    o_ref[...] = gx_ref[...] + norm_back(upstream, scaled, inverse, vec_ref[0:1, :])
    accumulate(
        sums_ref,
        jnp.concatenate([column_sum(upstream * scaled), column_sum(upstream)], axis=0),
    )


def input_back(lower, upper, rows, middle_grad, vec, weight, place):
    length = rows.shape[0]
    half = lower.shape[2]
    stacked = pl.BlockSpec((3, ROW_BLOCK, half), lambda i, *_: (0, i, 0))
    return weight_call(
        input_back_kernel,
        place,
        [(weight, 3 * D)],
        (length // ROW_BLOCK,),
        [stacked, stacked, row_spec(D), row_spec(D), whole(vec.shape)],
        [lower, upper, rows, middle_grad, vec],
        [row_spec(D), whole((2, D))],
        [shape((length, D), F32), shape((2, D), F32)],
        "input_back",
        2 * length * D * 3 * D,
        24e6,
    )


def narrow_kernel(place, a_ref, x1_ref, vec_ref, o_ref, buffer):
    o_ref[...] = x1_ref[...] + mxu(a_ref[...], buffer[...], NT) + vec_ref[11:12, :]


def narrow(active, middle, vec, weight, place):
    length, columns = active.shape
    return weight_call(
        narrow_kernel,
        place,
        [(weight, columns)],
        (length // ROW_BLOCK,),
        [row_spec(columns), row_spec(D), whole(vec.shape)],
        [active, middle, vec],
        [row_spec(D)],
        [shape((length, D), F32)],
        "narrow",
        2 * length * D * columns,
        26e6,
    )[0]


def gradient_kernel(cut, place, t_ref, t2_ref, r_ref, r2_ref, *refs):
    total = refs[-1]
    total[...] = (
        mxu(t_ref[...], r_ref[0], NN) + mxu(t2_ref[...], r2_ref[0], NN)
    ).astype(BF16)
    step, outs = pl.program_id(0), list(refs[:-1])
    z_count, _, rows, _ = outs[0].shape

    def share(send_ref, keep_ref, x_first):
        for z in range(z_count):
            for other in range(2):
                for ref, away in ((send_ref, True), (keep_ref, False)):
                    x = (1 - place[1] if away else place[1]) if x_first else other
                    y = other if x_first else (1 - place[2] if away else place[2])
                    first = pl.multiple_of(((2 * z + x) * 2 + y) * rows, rows)
                    ref[z, other] = total[pl.ds(first, rows), :]

    if cut:
        send, keep = outs[:2]
        outs = outs[2:]

        @pl.when(step < cut)
        def _():
            share(send, keep, True)

    if outs:

        @pl.when(step >= cut)
        def _():
            share(outs[0], outs[1], False)


def gradient(turned, turned_other, right, right_other, place, n_dp, x_tiles, tiles):
    groups, length, columns = right.shape
    half = columns // 2
    tile = groups * half // tiles
    steps = half // tile
    rows = D // n_dp // 2
    block = (n_dp // 2, 2, rows, tile)
    specs, shapes = [], []
    if x_tiles:
        specs += [pl.BlockSpec(block, lambda i, s: (0, 0, 0, jnp.minimum(i, x_tiles - 1)))] * 2
        shapes += [shape(block[:3] + (x_tiles * tile,), BF16)] * 2
    if x_tiles < tiles:
        specs += [pl.BlockSpec(block, lambda i, s: (0, 0, 0, jnp.maximum(i - x_tiles, 0)))] * 2
        shapes += [shape(block[:3] + ((tiles - x_tiles) * tile,), BF16)] * 2
    fixed = pl.BlockSpec((D, length), lambda i, s: (0, 0))
    return pl.pallas_call(
        partial(gradient_kernel, x_tiles),
        grid_spec=pltpu.PrefetchScalarGridSpec(
            num_scalar_prefetch=1,
            grid=(tiles,),
            in_specs=[
                fixed,
                fixed,
                pl.BlockSpec(
                    (1, length, tile),
                    lambda i, s: (i // steps, 0, s[3] * steps + lax.rem(i, steps)),
                ),
                pl.BlockSpec((1, length, tile), lambda i, s: (i // steps, 0, lax.rem(i, steps))),
            ],
            out_specs=specs,
            scratch_shapes=[pltpu.VMEM((D, tile), BF16)],
        ),
        out_shape=shapes,
        compiler_params=settings(GRADIENT_MIB),
        cost_estimate=cost(4 * D * length * groups * half, 14e6),
        name="gradient",
    )(place, turned, turned_other, right, right_other)


def wide_sum(*terms):
    return reduce(lambda a, b: a + b, [term.astype(F32) for term in terms])


def take(array, index, axis):
    return lax.dynamic_index_in_dim(array, index, axis, keepdims=False)


def near_free():
    return pl.CostEstimate(flops=1, bytes_accessed=1, transcendentals=0)


def assemble(place, arrays, shapes, moves):
    def body(place_ref, *refs):
        sems = refs[-1]
        copies = []
        for n, (source, at, target, to) in enumerate(moves):
            src, dst = refs[source], refs[len(arrays) + target]
            at = at(place_ref) if callable(at) else at
            copies.append(
                pltpu.make_async_copy(
                    src if at is None else src.at[at], dst if to is None else dst.at[to], sems.at[n]
                )
            )
        for copy in copies:
            copy.start()
        for copy in copies:
            copy.wait()

    return pl.pallas_call(
        body,
        grid_spec=pltpu.PrefetchScalarGridSpec(
            num_scalar_prefetch=1,
            grid=(1,),
            in_specs=[pl.BlockSpec(memory_space=pltpu.HBM)] * len(arrays),
            out_specs=[whole(dims) for dims in shapes],
            scratch_shapes=[pltpu.SemaphoreType.DMA((len(moves),))],
        ),
        out_shape=[shape(dims, BF16) for dims in shapes],
        compiler_params=settings(),
        cost_estimate=near_free(),
        name="assemble",
    )(place, *arrays)


def sums_of_two(place, pairs, axes):
    count = len(pairs)

    def body(place_ref, *refs):
        ins, outs = refs[: 2 * count], refs[2 * count : 3 * count]
        buffers, sems = refs[3 * count : 5 * count], refs[-1]
        copies = []
        for n in range(2 * count):
            away = 1 - place_ref[axes[n // 2]]
            copies.append(pltpu.make_async_copy(ins[n].at[:, away], buffers[n], sems.at[n]))
        for copy in copies:
            copy.start()
        for copy in copies:
            copy.wait()
        for n in range(count):
            kept, recv = buffers[2 * n], buffers[2 * n + 1]
            outs[n][...] = (kept[...].astype(F32) + recv[...].astype(F32)).astype(BF16)

    dims = [keep.shape[:1] + keep.shape[2:] for keep, _ in pairs]
    return pl.pallas_call(
        body,
        grid_spec=pltpu.PrefetchScalarGridSpec(
            num_scalar_prefetch=1,
            grid=(1,),
            in_specs=[pl.BlockSpec(memory_space=pltpu.HBM)] * (2 * count),
            out_specs=[whole(d) for d in dims],
            scratch_shapes=[pltpu.VMEM(d, BF16) for d in dims for _ in range(2)]
            + [pltpu.SemaphoreType.DMA((2 * count,))],
        ),
        out_shape=[shape(d, BF16) for d in dims],
        compiler_params=settings(),
        cost_estimate=near_free(),
        name="sums_of_two",
    )(place, *[array for pair in pairs for array in pair])


def sums_of_z(place, terms, axes, picks, recv=None):
    count = len(terms)
    widths = [keep.shape[3] for keep, _, _ in terms]
    rows, total = terms[0][0].shape[2], sum(widths)
    dtypes = [BF16, F32] if recv is not None else [BF16]
    dims = [(rows, total)] * 2 if recv is not None else [(len(picks), rows, total)]
    extra = [] if recv is None else [recv]

    def body(place_ref, *refs):
        ins = refs[: 3 * count]
        add = refs[3 * count : 3 * count + len(extra)]
        at = 3 * count + len(extra)
        outs, buffers, sems = refs[at : at + len(dims)], refs[at + len(dims) : -1], refs[-1]
        copies = []
        for p, (bits, _, _, _) in enumerate(picks):
            z = place_ref[0] ^ bits
            for n in range(3 * count):
                group, part = divmod(n, 3)
                source = ins[n].at[z] if part == 2 else ins[n].at[z, place_ref[axes[group]]]
                copies.append(
                    pltpu.make_async_copy(source, buffers[group].at[p, part], sems.at[len(copies)])
                )
        for copy in copies:
            copy.start()
        for copy in copies:
            copy.wait()
        for p, (_, added, out, row) in enumerate(picks):
            first = 0
            for group, width in enumerate(widths):
                columns = slice(first, first + width)
                first += width
                value = wide_sum(*[buffers[group][p, part] for part in range(3)])
                if added is not None:
                    value = value + add[0][added, :, columns].astype(F32)
                if row is None:
                    outs[out][:, columns] = value.astype(dtypes[out])
                else:
                    outs[out][row, :, columns] = value.astype(dtypes[out])

    return pl.pallas_call(
        body,
        grid_spec=pltpu.PrefetchScalarGridSpec(
            num_scalar_prefetch=1,
            grid=(1,),
            in_specs=[pl.BlockSpec(memory_space=pltpu.HBM)] * (3 * count)
            + [whole(array.shape) for array in extra],
            out_specs=[whole(d) for d in dims],
            scratch_shapes=[pltpu.VMEM((len(picks), 3, rows, width), BF16) for width in widths]
            + [pltpu.SemaphoreType.DMA((len(picks) * 3 * count,))],
        ),
        out_shape=[shape(d, dtype) for d, dtype in zip(dims, dtypes)],
        compiler_params=settings(),
        cost_estimate=near_free(),
        name="sums_of_z",
    )(place, *[array for term in terms for array in term], *extra)


def finish(halves, before=None):
    widths = [total.shape[1] for total, _ in halves]
    rows = halves[0][0].shape[0]
    extra = [] if before is None else [before]

    def body(*refs):
        out, squares = refs[-2:]
        result = refs[2 * len(halves)][...] if extra else jnp.zeros((1, 128), F32)
        first = 0
        for n, width in enumerate(widths):
            value = refs[2 * n][...] + refs[2 * n + 1][...].astype(F32)
            out[:, first : first + width] = value.astype(BF16)
            first += width
            result = result + jnp.sum(value * value)
        squares[...] = result

    return pl.pallas_call(
        body,
        out_shape=[shape((rows, sum(widths)), BF16), shape((1, 128), F32)],
        compiler_params=settings(),
        cost_estimate=near_free(),
        name="finish",
    )(*[array for half in halves for array in half], *extra)


def adam_step(weight, grad, first, second, rate, decay):
    first_next = BETA_ONE * first + (1.0 - BETA_ONE) * grad
    second_next = BETA_TWO * second + (1.0 - BETA_TWO) * grad * grad
    first_hat = first_next / (1.0 - BETA_ONE**STEP)
    second_hat = second_next / (1.0 - BETA_TWO**STEP)
    weight_next = weight - rate * (first_hat / (jnp.sqrt(second_hat) + ADAM_EPS) + decay * weight)
    return (weight_next, first_next, second_next)


def adam_kernel(halves, groups, place, factor, *refs):
    pieces, rest = refs[: 4 * groups], refs[4 * groups :]
    w_ref, m_ref, s_ref, wn_ref, mn_ref, sn_ref, half_ref = rest
    height, width = pieces[0].shape
    step = pl.program_id(0)

    def update(group, core, y, columns):
        choice = (core ^ place[3]) * 2 + (y ^ place[2])
        rows = slice(y * height, (y + 1) * height)
        grad = pieces[4 * group][...]
        for k in (1, 2, 3):
            grad = jnp.where(choice == k, pieces[4 * group + k][...], grad)
        new = adam_step(
            w_ref[rows, columns],
            grad.astype(F32) * factor[0],
            m_ref[rows, columns],
            s_ref[rows, columns],
            MATRIX_RATE,
            DECAY,
        )
        wn_ref[rows, columns], mn_ref[rows, columns], sn_ref[rows, columns] = new
        half_ref[rows, columns] = new[0].astype(BF16)

    for y in range(2):
        if halves == 1:
            update(0, step // 2, y, slice(None))
        else:
            for group in range(groups):

                @pl.when(lax.rem(step, groups) == group)
                def _(group=group):
                    for core in range(2):
                        update(group, core, y, slice(core * width, (core + 1) * width))


def adam(place, factor, pieces, starts, weight, first, second):
    rows, columns = weight.shape
    groups = len(starts)
    if groups == 1:
        steps, tile = 4, columns // 4
        width = tile
        specs = [
            pl.BlockSpec((rows // 2, width), lambda i, *_: (0, starts[0] // width + lax.rem(i, 2)))
        ] * 4
    else:
        steps, tile = columns // 512, 512
        width = tile // 2
        specs = [
            pl.BlockSpec(
                (rows // 2, width), lambda i, *_, start=start: (0, start // width + i // groups)
            )
            for start in starts
            for _ in range(4)
        ]
    block = pl.BlockSpec((rows, tile), lambda i, *_: (0, i))
    full = (rows, columns)
    return pl.pallas_call(
        partial(adam_kernel, tile // width, groups),
        grid_spec=pltpu.PrefetchScalarGridSpec(
            num_scalar_prefetch=2,
            grid=(steps,),
            in_specs=specs + [block] * 3,
            out_specs=[block] * 4,
        ),
        out_shape=[shape(full, F32)] * 3 + [shape(full, BF16)],
        compiler_params=settings(20),
        cost_estimate=cost(0, rows * columns * 28),
        name="adam",
    )(place, factor, *(pieces * groups), weight, first, second)


def tied(values, *others):
    return lax.optimization_barrier((values,) + others)[0]


KERNELS = (
    turn,
    first_norm,
    project,
    attend_forward,
    join,
    widen_half,
    hidden_back,
    middle_back,
    attend_backward,
    gradient,
    input_back,
    narrow,
)


class Order:
    def __init__(self):
        self.last = []
        self.pending = []

    def __call__(self, work, *operands):
        if self.last:
            leaves, tree = jax.tree_util.tree_flatten(operands)
            arrays = [leaf for leaf in leaves if isinstance(leaf, jax.Array)]
            if work in KERNELS:
                arrays[0] = tied(arrays[0], *self.last, *self.pending)
            else:
                arrays = lax.optimization_barrier((*arrays, *self.last, *self.pending))
            arrays = iter(arrays)
            leaves = [next(arrays) if isinstance(leaf, jax.Array) else leaf for leaf in leaves]
            operands = jax.tree_util.tree_unflatten(tree, leaves)
        result = work(*operands)
        self.last, self.pending = jax.tree_util.tree_leaves(result), []
        return result

    def send(self, array, **bits):
        return swap(tied(array, *self.last), **bits)

    def land(self, *arrays):
        self.pending += arrays

    def cross(self, array):
        crossed = swap(tied(array, *self.last, *self.pending), core=1)
        return crossed

    def cross_all(self, *arrays):
        crossed = [self.cross(array) for array in arrays]
        self.pending += crossed
        return crossed


def stack_z(*parts):
    return jnp.stack(parts)


def to_send(own, place, parts, split_y, extra=None):
    mine = pack(own, place, parts, split_y).astype(BF16)
    if extra is None:
        return mine
    flat = extra.astype(BF16).reshape(-1, mine.shape[1])
    spare = -(mine.shape[0] + flat.shape[0]) % 16
    return jnp.concatenate([mine, flat, jnp.zeros((spare, mine.shape[1]), BF16)], axis=0)


def vectors_of(near, far, index, rows, dims, n_dp):
    count = dims[0] * dims[1] // near.shape[2]
    both = jnp.stack([near[:, rows : rows + count], far[:, rows : rows + count]], axis=1)
    both = both.reshape((n_dp,) + dims)
    return jnp.concatenate([take(both, index ^ j, 0) for j in range(n_dp)], axis=1).astype(F32)


def per_device(
    tokens,
    segment_ids,
    cotangent,
    qkv_weight,
    out_weight,
    up_weight,
    down_weight,
    vectors,
    qkv_first,
    qkv_second,
    out_first,
    out_second,
    up_first,
    up_second,
    down_first,
    down_second,
    vectors_first,
    vectors_second,
):
    n_dp, n_rep = lax.axis_size("dp"), lax.axis_size("rep")
    paired = n_dp == 8 and n_rep == 4
    dp, rep = lax.axis_index("dp"), lax.axis_index("rep")
    z, x, y, core = dp // 2, dp % 2, rep // 2, rep % 2
    place = jnp.stack([z, x, y, core]).astype(jnp.int32)
    seq_len = tokens.shape[1]
    segs_column = segment_ids.reshape(seq_len, 1)
    rows = tokens.reshape(seq_len, D)
    cot = cotangent.reshape(seq_len, D)
    up_rows = FF // D
    shard = qkv_weight.shape[0]
    masters = (qkv_weight, out_weight, up_weight, down_weight, vectors)
    pairs = HEADS // 2
    run = Order()

    if paired:

        def held(zs, here, x=0, y=0, there=None):
            return [(here, zs, x, y, 0), (there, zs, x, y, 1)]

        def all_z(mine):
            return [run.send(mine, z=bits) for bits in (1, 2, 3)]

        half, b_two = FF // 2, 3 * D // 4
        straight, zs = (0, 1, 2, 3), (0, 2, 1, 3)
        mine_b = to_send(qkv_weight, place, [(0, D, D // 2)], True, vectors)
        near_b = [swap(mine_b, z=bits) for bits in (1, 2, 3)]
        run.last = [mine_b]
        mine_a = run(to_send, qkv_weight, place, [(2 * D, D // 2, D // 2)], False)
        mine_two = run(
            lambda up, out: jnp.concatenate(
                [
                    pack(up, place, [(D // 2, half, b_two)], True),
                    pack(out, place, [(0, D // 2, D // 2)], False),
                ],
                axis=1,
            ).astype(BF16),
            up_weight,
            out_weight,
        )
        mine_three = run(to_send, down_weight, place, [(0, half, half // 2)], True)
        mine_last = run(to_send, up_weight, place, [(0, half, D // 2)], False)
        stack_b = run(stack_z, mine_b, *near_b)
        far_b, side_b = run.send(stack_b, x=1), run.send(stack_b, y=1)
        near_a = all_z(mine_a)
        cot_turned, down_bias_grad = run(turn, cot)
        run.land(far_b, side_b)
        vec = run(vectors_of, stack_b, far_b, dp, shard, vectors.shape, n_dp)
        across_b = run.send(far_b, y=1)
        stack_a = run(stack_z, mine_a, *near_a)
        far_a, far_two = run.send(stack_a, x=1), run.send(mine_two, z=2)
        near_b_other, far_b_other = run.send(stack_b, core=1), run.send(far_b, core=1)
        normed_one, normed_one_turned, scale_sum = run(first_norm, rows, vec)
        run.land(near_b_other, far_b_other, across_b, far_a, far_two)
        side_b_other, across_b_other, near_a_other, far_a_other = run.cross_all(
            side_b, across_b, stack_a, far_a
        )
        pair_two = run(stack_z, mine_two, far_two)
        other_two = run.send(pair_two, z=1)
        normed_one_turned_other = run.send(normed_one_turned, core=1)
        cot_turned_other = run.send(cot_turned, core=1)
        qkv_all = gathered(
            shard,
            held(straight, stack_b, there=near_b_other)
            + held(straight, far_b, 1, there=far_b_other)
            + held(straight, side_b, 0, 1, side_b_other)
            + held(straight, across_b, 1, 1, across_b_other),
            0,
            D // 2,
            0,
            D,
            D // 2,
        ) + gathered(
            shard,
            held(straight, stack_a, there=near_a_other) + held(straight, far_a, 1, there=far_a_other),
            0,
            D // 2,
            2 * D,
            D // 2,
            0,
        )
    else:
        vec = lax.all_gather(vectors.astype(BF16), "dp", axis=1, tiled=True).astype(F32)
        low = qkv_weight.astype(BF16)
        qkv_all = whole_rows(low)
        out_all, up_all, down_all = (
            whole_rows(own.astype(BF16)) for own in (out_weight, up_weight, down_weight)
        )
        cot_turned, down_bias_grad = run(turn, cot)
        normed_one, normed_one_turned, scale_sum = run(first_norm, rows, vec)

    qkv_bias = jnp.concatenate([vec[2:3], jnp.zeros((1, D), F32), vec[3:4]], axis=1)
    qkv = run(project, normed_one, qkv_bias, qkv_all, place)
    if paired:
        run.land(normed_one_turned_other, cot_turned_other)
        stack_b, stack_a = run(
            lambda *t: assemble(
                place,
                t,
                [(4, shard, b_two), (4, shard, D // 2)],
                [
                    (n, (slice(0, 2), slice(None), columns), out, slice(2 * n, 2 * n + 2))
                    for n in range(2)
                    for out, columns in ((0, slice(0, b_two)), (1, slice(b_two, b_two + D // 2)))
                ],
            ),
            pair_two,
            other_two,
        )
        far_b, side_b = run.send(stack_b, x=1), run.send(stack_b, y=1)
        far_last, far_three = run.send(mine_last, z=2), run.send(mine_three, z=2)
        near_a_other = run.send(stack_a, core=1)
    context, lower_sums = run(attend_forward, qkv, segment_ids, segs_column, 0, pairs // 2)
    if paired:
        run.land(far_b, side_b, near_a_other)
        pair_last, pair_three = run(
            lambda *t: assemble(
                place,
                t,
                [(2, shard, D // 2), (2, shard, half // 2)],
                [(n, None, n // 2, n % 2) for n in range(4)],
            ),
            mine_last,
            far_last,
            mine_three,
            far_three,
        )
        across_b, far_a = run.send(far_b, y=1), run.send(stack_a, x=1)
        other_last, other_three = run.send(pair_last, z=1), run.send(pair_three, z=1)
        near_b_other = run.send(stack_b, core=1)
    context, upper_sums = run(attend_forward, qkv, segment_ids, segs_column, pairs // 2, pairs // 2, context)
    if paired:
        run.land(across_b, far_a, near_b_other, other_last, other_three)
        [far_a_other] = run.cross_all(far_a)

        def other_half(s):
            start = pl.multiple_of((1 - s[3]) * (D // 2), D // 2)
            return (slice(None), pl.ds(start, D // 2))

        stack_last, stack_three, context_send = run(
            lambda *t: assemble(
                place,
                t,
                [(4, shard, D // 2), (4, shard, half // 2), (seq_len, D // 2)],
                [(n, None, n // 2, slice(n % 2 * 2, n % 2 * 2 + 2)) for n in range(4)]
                + [(4, other_half, 2, None)],
            ),
            pair_last,
            other_last,
            pair_three,
            other_three,
            context,
        )
        a_held = held(zs, stack_a, there=near_a_other) + held(zs, far_a, 1, there=far_a_other)
        out_all = gathered(shard, a_held, 0, D // 2, 0, D // 2, 0)
        far_last = run.send(stack_last, x=1)
        side_b_other, far_b_other = run.send(side_b, core=1), run.send(far_b, core=1)
        across_b_other, near_last_other = run.send(across_b, core=1), run.send(stack_last, core=1)
    middle, normed_two, normed_two_turned = run(join, context, rows, vec, out_all, place)
    up_bias = vec[7 : 7 + up_rows].reshape(1, FF)
    if paired:
        run.land(side_b_other, far_b_other, across_b_other, near_last_other, far_last)
        [far_last_other] = run.cross_all(far_last)
        far_three, side_three = run.send(stack_three, x=1), run.send(stack_three, y=1)
        normed_two_turned_other = run.send(normed_two_turned, core=1)
        context_other = run.send(context_send, core=1)
        near_three_other = run.send(stack_three, core=1)
        b_held = (
            held(zs, stack_b, there=near_b_other)
            + held(zs, far_b, 1, there=far_b_other)
            + held(zs, side_b, 0, 1, side_b_other)
            + held(zs, across_b, 1, 1, across_b_other)
        )
        last_held = held(zs, stack_last, there=near_last_other) + held(
            zs, far_last, 1, there=far_last_other
        )
        def up_of(b_held, last_held, core_step):
            return gathered(shard, b_held, 0, b_two, D // 2, core_step, b_two) + gathered(
                shard, last_held, 0, D // 2, 0, core_step, 0
            )

        up_all = up_of(b_held, last_held, half)
        up_there, up_here = (
            up_of([t for t in b_held if t[4] == c], [t for t in last_held if t[4] == c], 0)
            for c in (1, 0)
        )
    else:
        up_there, up_here = (
            [(lax.dynamic_slice_in_dim(up_all[0][0], c * (FF // 2), FF // 2, 1), [up_all[0][1][0][:6] + (FF // 2, 0, 0, 0)])]
            for c in (1 - core, core)
        )
    active, slope, active_send = run(widen_half, normed_two, up_bias, up_there, place)
    if paired:
        run.land(far_three, side_three, normed_two_turned_other, context_other, near_three_other)
        across_three = run.send(far_three, y=1)
        active_other = run.send(active_send, core=1)
        far_three_other, side_three_other = run.send(far_three, core=1), run.send(side_three, core=1)
    active, slope = run(widen_half, normed_two, up_bias, up_here, place, (active, slope))

    if not paired:

        def product(turned, right):
            groups = [
                jnp.dot(turned, right[g], preferred_element_type=F32) for g in range(right.shape[0])
            ]
            return jnp.concatenate(groups, axis=1)

        grad_down = product(cot_turned, active[None])
        hidden_grad, _, up_bias_grad = hidden_back(cot, slope, down_all, place)
        grad_up = product(normed_two_turned, hidden_grad[None])
        middle_grad, branch_grad, branch_turned, context_grad, middle_sums = middle_back(
            hidden_grad, middle, cot, vec, up_all, out_all, place
        )
        grad_out = product(branch_turned, context[None])
        lower, _, lower_bias = attend_backward(
            qkv, segment_ids, segs_column, context_grad, lower_sums, 0, pairs // 2, place
        )
        upper, _, upper_bias = attend_backward(
            qkv, segment_ids, segs_column, context_grad, upper_sums, pairs // 2, pairs // 2, place
        )
        parts = [product(normed_one_turned, grads) for grads in (lower, upper)]
        parts = [[part[:, j * D // 2 : (j + 1) * D // 2] for j in range(3)] for part in parts]
        grad_qkv = jnp.concatenate([t for pair in zip(*parts) for t in pair], axis=1)
    else:


        def cut(turned, right, x_tiles, tiles):
            outs = run(gradient, *turned, *right, place, n_dp, x_tiles, tiles)
            parts = []
            if x_tiles:
                parts.append((outs[1], run.send(outs[0], x=1), 2, {"y": 1}))
            if x_tiles < tiles:
                parts.append((outs[-1], run.send(outs[-2], y=1), 1, {"x": 1}))
            return parts

        def cut_again(parts):
            sends = run(
                lambda pairs: sums_of_two(place, pairs, [part[2] for part in parts]),
                [part[:2] for part in parts],
            )
            return [
                (keep, recv, run.send(send, **way), axis)
                for (keep, recv, axis, way), send in zip(parts, sends)
            ]

        def along_z(terms):
            axes = [term[3] for term in terms]
            [send] = run(
                lambda t: sums_of_z(place, t, axes, [(1, None, 0, 0), (3, None, 0, 1)]),
                [term[:3] for term in terms],
            )
            return terms, run.send(send, z=1)

        def along_z_again(terms, recv):
            axes = [term[3] for term in terms]
            send, total = run(
                lambda t, r: sums_of_z(place, t, axes, [(2, 1, 0, None), (0, 0, 1, None)], r),
                [term[:3] for term in terms],
                recv,
            )
            return total, run.send(send, z=2)

        run.land(active_other, far_three_other, side_three_other)
        cut_down = cut((cot_turned, cot_turned_other), (active[None], active_other[None]), 2, 4)
        run.land(across_three)
        [across_three_other] = run.cross_all(across_three)
        down_all = gathered(
            shard,
            held(zs, stack_three, there=near_three_other)
            + held(zs, far_three, 1, there=far_three_other)
            + held(zs, side_three, 0, 1, side_three_other)
            + held(zs, across_three, 1, 1, across_three_other),
            0,
            FF // 4,
            0,
            half,
            FF // 4,
        )
        hidden_grad, hidden_send, up_bias_grad = run(hidden_back, cot, slope, down_all, place)
        terms_down = cut_again(cut_down)
        hidden_other = run.send(hidden_send, core=1)
        middle_grad, branch_grad, branch_turned, context_grad, middle_sums = run(
            middle_back, hidden_grad, middle, cot, vec, up_all, out_all, place
        )
        run.land(hidden_other)
        z_down = along_z(terms_down)
        branch_turned_other = run.send(branch_turned, core=1)
        cut_up = cut(
            (normed_two_turned, normed_two_turned_other), (hidden_grad[None], hidden_other[None]), 2, 4
        )
        run.land(branch_turned_other)
        half_down = along_z_again(*z_down)
        lower, lower_send, lower_bias = run(
            attend_backward, qkv, segment_ids, segs_column, context_grad, lower_sums, 0, pairs // 2, place
        )
        run.land(half_down[1])
        terms_up = cut_again(cut_up)
        lower_other = run.send(lower_send, core=1)
        cut_out = cut((branch_turned, branch_turned_other), (context[None], context_other[None]), 0, 1)
        run.land(lower_other)
        upper, upper_send, upper_bias = run(
            attend_backward,
            qkv,
            segment_ids,
            segs_column,
            context_grad,
            upper_sums,
            pairs // 2,
            pairs // 2,
            place,
        )
        terms_out = cut_again(cut_out)
        upper_other = run.send(upper_send, core=1)
        turned_pair = (normed_one_turned, normed_one_turned_other)
        cut_lower = cut(turned_pair, (lower, lower_other), 1, 3)
        run.land(terms_out[0][2], upper_other)
        cut_upper = cut(turned_pair, (upper, upper_other), 2, 3)
        z_up = along_z(terms_up)
    input_grad, input_sums = run(
        input_back, lower, upper, rows, middle_grad, vec, qkv_all, place
    )
    grad_vec = jnp.concatenate(
        [
            input_sums,
            jnp.concatenate([lower_bias, upper_bias], axis=1),
            middle_sums,
            up_bias_grad.reshape(up_rows, D),
            down_bias_grad,
            jnp.broadcast_to(scale_sum[:, :1], (1, D)),
        ],
        axis=0,
    )
    if paired:
        run.land(*[part[1] for part in cut_lower + cut_upper])
        [vec_recv] = run.cross_all(grad_vec)
        grad_vec = grad_vec + vec_recv
        terms_last = cut_again(cut_lower + cut_upper)
        half_up = along_z_again(*z_up)
    if paired:
        z_late = along_z(terms_out + terms_last)
        vec_recv = run.send(grad_vec, y=1)
    block_out = run(narrow, active, middle, vec, down_all, place)
    if paired:
        early, squares = run(finish, [half_down, half_up])
        early_other = run.send(early, y=1)
        half_late = along_z_again(*z_late)
        for bits in ({"x": 1}, {"z": 1}):
            grad_vec = run(lambda a, b: a + b, grad_vec, vec_recv)
            vec_recv = run.send(grad_vec, **bits)
        grad_vec = run(lambda a, b: a + b, grad_vec, vec_recv)
        vec_recv = run.send(grad_vec, z=2)
    total_rows = seq_len * n_dp * n_rep
    firsts = (qkv_first, out_first, up_first, down_first)
    seconds = (qkv_second, out_second, up_second, down_second)
    if paired:
        late, squares = run(finish, [half_late], squares)
        squares = squares + swap(squares, core=1)
        squares = squares + swap(squares, y=1)
        late_other = swap(tied(late, squares), y=1)
        for bits in ({"x": 1}, {"z": 1}, {"z": 2}):
            squares = squares + swap(squares, **bits)
        squares = squares[0, 0]
        grad_vec = grad_vec + vec_recv
    else:
        shards = [
            lax.psum(lax.psum_scatter(grad, "dp", scatter_dimension=0, tiled=True), "rep")
            for grad in (grad_qkv, grad_out, grad_up, grad_down)
        ]
        grad_vec = lax.psum(grad_vec, AXES)
        squares = lax.psum(reduce(lambda a, b: a + b, [jnp.sum(p * p) for p in shards]), "dp")
    input_scale = grad_vec[12, 0] / total_rows
    grad_vec = grad_vec[:12]
    grad_norm = jnp.sqrt(squares + jnp.sum(grad_vec * grad_vec))
    clip_factor = jnp.minimum(1.0, CLIP_NORM / (grad_norm + 1e-06))
    updates = []
    if paired:
        early = [early, early_other, swap(early, core=1), swap(early_other, core=1)]
        late = [late, late_other, swap(late, core=1), swap(late_other, core=1)]
        factor = clip_factor.reshape(1)
        sources = [
            (late, [D // 2, D // 2 + 3 * D // 4]),
            (late, [0]),
            (early, [half]),
            (early, [0]),
        ]
        for (pieces, starts), weight, first, second in zip(sources, masters, firsts, seconds):
            updates.append(adam(place, factor, pieces, starts, weight, first, second))
    else:
        for grad, weight, first, second in zip(shards, masters, firsts, seconds):
            new = adam_step(weight, grad * clip_factor, first, second, MATRIX_RATE, DECAY)
            updates.append(new + (new[0].astype(BF16),))
    width = vectors.shape[1]
    vec_shard = lax.dynamic_slice_in_dim(grad_vec, dp * width, width, 1)
    new = adam_step(
        vectors, vec_shard * clip_factor, vectors_first, vectors_second, VECTOR_RATE, 0.0
    )
    updates.append(new + (new[0].astype(BF16),))
    return (
        (
            block_out.reshape(1, seq_len, D),
            input_grad.reshape(1, seq_len, D),
            grad_norm,
            input_scale,
        )
        + tuple(update[0] for update in updates)
        + tuple(update[1] for update in updates)
        + tuple(update[2] for update in updates)
        + tuple(update[3] for update in updates)
    )


def solution(mesh):
    rows = P(("dp", "rep"), None, None)
    matrix, vector = P("dp", None), P(None, "dp")
    weights = (matrix,) * 4 + (vector,)
    return jax.shard_map(
        per_device,
        mesh=mesh,
        in_specs=(rows, P(("dp", "rep"), None), rows)
        + weights
        + (matrix,) * 8
        + (vector,) * 2,
        out_specs=(rows, rows, P(), P()) + weights * 4,
        check_vma=False,
    )
```

```python
from functools import partial
from functools import reduce
import math

import jax
import jax.numpy as jnp
from jax import lax
from jax.experimental import pallas as pl
from jax.experimental.pallas import tpu as pltpu
from jax.sharding import PartitionSpec as P

HEADS = 16
HEAD_DIM = 64
D = 1024
FF = 4096
STEP = 10


LN_EPS = 1e-05
CLIP_NORM = 1.0
BETA_ONE = 0.9
BETA_TWO = 0.95
ADAM_EPS = 1e-08
MATRIX_RATE = 0.1
VECTOR_RATE = 1.0
DECAY = 0.1
MASKED = -1e30

F32 = jnp.float32
BF16 = jnp.bfloat16
AXES = ("dp", "rep")
MIB = 2**20
NN = (((1,), (0,)), ((), ()))
NT = (((1,), (1,)), ((), ()))
TN = (((0,), (0,)), ((), ()))


def mxu(left, right, dims):
    return lax.dot_general(left, right, dims, preferred_element_type=F32)


def shape(dims, dtype):
    return jax.ShapeDtypeStruct(dims, dtype)


def settings(mib=56):
    return pltpu.CompilerParams(vmem_limit_bytes=mib * MIB)


SCALE = 50


def cost(flops, moved):
    return pl.CostEstimate(flops=int(SCALE * flops), bytes_accessed=int(SCALE * moved), transcendentals=0)


def swap(values, z=0, x=0, y=0, core=0):
    n_dp, n_rep = lax.axis_size("dp"), lax.axis_size("rep")
    dp_bits, rep_bits = 2 * z + x, 2 * y + core
    pairs = [
        (dp * n_rep + rep, (dp ^ dp_bits) * n_rep + (rep ^ rep_bits))
        for dp in range(n_dp)
        for rep in range(n_rep)
    ]
    return lax.ppermute(values, AXES, pairs)


def pack(own, place, parts, split_y):
    mine = []
    for low, core_step, width in parts:
        start = low + place[3] * core_step + (place[2] * width if split_y else 0)
        mine.append(lax.dynamic_slice_in_dim(own, start, width, 1))
    return mine[0] if len(mine) == 1 else jnp.concatenate(mine, axis=1)


def gathered(rows, stacks, column, width, target, half, y_step):
    return [
        (array, [(z, x, y, core, rows, column, width, target, half, y_step) for z in zs])
        for array, zs, x, y, core in stacks
    ]


def whole_rows(own):
    full = lax.all_gather(own, "dp", axis=0, tiled=True)
    return [(full, [(0, 0, 0, 0, full.shape[0], 0, full.shape[1], 0, 0, 0)])]


def piece_copies(place, ref, plan, target, sems, first):
    copies, at = [], None
    for i, (z, x, y, core, rows, column, width, start, half, y_step) in enumerate(plan):
        if len(ref.shape) == 3:
            row = pl.multiple_of(((place[0] ^ z) * 2 + (place[1] ^ x)) * rows, rows)
            at = start + (place[3] ^ core) * half + (place[2] ^ y) * y_step
            column_at = pl.multiple_of(at, 128)
            source = ref.at[i, pl.ds(0, rows), pl.ds(column, width)]
        else:
            row, column_at, source = 0, start, ref
        copies.append(
            pltpu.make_async_copy(
                source, target.at[pl.ds(row, rows), pl.ds(column_at, width)], sems.at[first + i]
            )
        )
    return at, copies


def turned_step(place, steps):
    half = steps // 2
    return lambda i, *_: lax.rem((1 - place[3]) * half + i, steps)


QUERY_BLOCK = 128
KEY_SPAN = 512


def bands(length):
    return [
        (b * QUERY_BLOCK, max(0, b * QUERY_BLOCK - KEY_SPAN), (b + 1) * QUERY_BLOCK)
        for b in range(length // QUERY_BLOCK)
    ]


def head_slope(head):
    return jnp.exp2(-8.0 * (head.astype(F32) + 1.0) / HEADS)


def head_lanes(h):
    lane = lax.broadcasted_iota(jnp.int32, (1, 2 * HEAD_DIM), 1)
    return (lane >= HEAD_DIM) if h else (lane < HEAD_DIM)


def both_heads(rows):
    return jnp.concatenate([jnp.where(head_lanes(h), rows, BF16(0)) for h in range(2)], axis=0)


def own_lanes(rows):
    half = rows.shape[0] // 2
    return jnp.where(head_lanes(0), rows[:half], rows[half:])


def fill_base(segs_row, segs_column, base, length):
    for b, (first, low, high) in enumerate(bands(length)):
        keys = low + lax.broadcasted_iota(jnp.int32, (high - low, QUERY_BLOCK), 0)
        rows = first + lax.broadcasted_iota(jnp.int32, (high - low, QUERY_BLOCK), 1)
        allowed = (keys <= rows) & (
            segs_column[low:high, :] == segs_row[:, first : first + QUERY_BLOCK]
        )
        base[b, : high - low, :] = jnp.where(allowed, (keys - rows).astype(F32), MASKED)


def biased(scores, base, pair):
    return jnp.concatenate(
        [
            scores[:, h * QUERY_BLOCK : (h + 1) * QUERY_BLOCK] + head_slope(2 * pair + h) * base
            for h in range(2)
        ],
        axis=1,
    )


def attend_forward_kernel(
    first_pair, segs_row, segs_column, q_ref, k_ref, v_ref, *refs
):
    c_ref, lse_ref, base = refs[-3:]
    length = q_ref.shape[0]

    @pl.when(pl.program_id(0) == 0)
    def _():
        fill_base(segs_row, segs_column, base, length)

    pair = first_pair + pl.program_id(0)
    for b, (first, low, high) in enumerate(bands(length)):
        rows = slice(first, first + QUERY_BLOCK)
        queries, keys, values = q_ref[rows, :], k_ref[low:high, :], v_ref[low:high, :]
        scaled = both_heads(queries * BF16(1.0 / math.sqrt(HEAD_DIM)))
        scores = biased(mxu(keys, scaled, NT), base[b, : high - low, :], pair)
        top = jnp.max(scores, axis=0, keepdims=True)
        weights = jnp.exp(scores - top)
        total = jnp.sum(weights, axis=0, keepdims=True)
        probs = (weights * (1.0 / total)).astype(BF16)
        c_ref[rows, :] = own_lanes(mxu(probs, values, TN)).astype(BF16)
        lse = top + jnp.log(total)
        for h in range(2):
            lse_ref[0, h : h + 1, rows] = lse[:, h * QUERY_BLOCK : (h + 1) * QUERY_BLOCK]


def attend_forward(qkv, segs, segs_column, first_pair, pairs, context=None):
    length, width = qkv.shape[0], 2 * HEAD_DIM
    per = D // width
    before = [] if context is None else [context]
    return pl.pallas_call(
        partial(attend_forward_kernel, first_pair),
        grid=(pairs,),
        in_specs=[
            pl.BlockSpec((1, length), lambda i: (0, 0)),
            pl.BlockSpec((length, 1), lambda i: (0, 0)),
            pl.BlockSpec((length, width), lambda i: (0, first_pair + i)),
            pl.BlockSpec((length, width), lambda i: (0, per + first_pair + i)),
            pl.BlockSpec((length, width), lambda i: (0, 2 * per + first_pair + i)),
        ]
        + [pl.BlockSpec(memory_space=pltpu.HBM)] * len(before),
        out_specs=[
            pl.BlockSpec((length, width), lambda i: (0, first_pair + i)),
            pl.BlockSpec((1, 2, length), lambda i: (i, 0, 0)),
        ],
        input_output_aliases={5: 0} if before else {},
        out_shape=[
            shape((length, D), BF16),
            shape((pairs, 2, length), F32),
        ],
        scratch_shapes=[pltpu.VMEM((length // QUERY_BLOCK, KEY_SPAN + QUERY_BLOCK, QUERY_BLOCK), F32)],
        compiler_params=settings(),
        cost_estimate=cost(3.5e9 * pairs, 1e6 * pairs),
        name="attend_forward",
    )(segs, segs_column, qkv, qkv, qkv, *before)


def attend_backward_kernel(
    first_pair,
    pairs,
    place,
    segs_row,
    segs_column,
    q_ref,
    k_ref,
    v_ref,
    g_ref,
    lse_ref,
    o_ref,
    send_ref,
    sums_ref,
    base,
    dk,
    dv,
):
    length = q_ref.shape[0]

    @pl.when(pl.program_id(0) == 0)
    def _():
        fill_base(segs_row, segs_column, base, length)

    pair = first_pair + turned_step(place, pairs)(pl.program_id(0))
    dk[...] = jnp.zeros_like(dk)
    dv[...] = jnp.zeros_like(dv)
    query_sum = jnp.zeros((1, 2 * HEAD_DIM), F32)
    inv_root = BF16(1.0 / math.sqrt(HEAD_DIM))
    for b, (first, low, high) in enumerate(bands(length)):
        rows = slice(first, first + QUERY_BLOCK)
        keys, values = k_ref[low:high, :], v_ref[low:high, :]
        queries, grads = both_heads(q_ref[rows, :]), both_heads(g_ref[rows, :])
        scores = biased(mxu(keys, queries * inv_root, NT), base[b, : high - low, :], pair)
        lse = jnp.concatenate([lse_ref[0, h : h + 1, rows] for h in range(2)], axis=1)
        probs = jnp.exp(scores - lse)
        prob_grad = mxu(values, grads * inv_root, NT)
        row_dot = jnp.sum(probs * prob_grad, axis=0, keepdims=True)
        score_grad = (probs * (prob_grad - row_dot)).astype(BF16)
        dv[low:high, :] += mxu(probs.astype(BF16), grads, NN)
        dk[low:high, :] += mxu(score_grad, queries, NN)
        dq = own_lanes(mxu(score_grad, keys, TN)).astype(BF16)
        o_ref[0, rows, :] = dq
        query_sum = query_sum + jnp.sum(dq.astype(F32), axis=0, keepdims=True)
    o_ref[1] = dk[...].astype(BF16)
    value_grad = dv[...].astype(BF16)
    o_ref[2] = value_grad
    sums_ref[0:1, :] = query_sum
    sums_ref[1:2, :] = jnp.sum(value_grad.astype(F32), axis=0, keepdims=True)

    @pl.when(pl.program_id(0) < pairs // 2)
    def _():
        send_ref[...] = o_ref[...]


def attend_backward(qkv, segs, segs_column, grads, lse, first_pair, pairs, place):
    length, width = qkv.shape[0], 2 * HEAD_DIM
    per = D // width

    def heads(first):
        return pl.BlockSpec(
            (length, width), lambda i, s: (0, first + first_pair + turned_step(s, pairs)(i))
        )

    return pl.pallas_call(
        partial(attend_backward_kernel, first_pair, pairs),
        grid_spec=pltpu.PrefetchScalarGridSpec(
            num_scalar_prefetch=1,
            grid=(pairs,),
            in_specs=[
                pl.BlockSpec((1, length), lambda i, s: (0, 0)),
                pl.BlockSpec((length, 1), lambda i, s: (0, 0)),
                heads(0),
                heads(per),
                heads(2 * per),
                heads(0),
                pl.BlockSpec((1, 2, length), lambda i, s: (turned_step(s, pairs)(i), 0, 0)),
            ],
            out_specs=[
                pl.BlockSpec((3, length, width), lambda i, s: (0, 0, turned_step(s, pairs)(i))),
                pl.BlockSpec((3, length, width), lambda i, s: (0, 0, jnp.minimum(i, pairs // 2 - 1))),
                pl.BlockSpec((2, width), lambda i, s: (0, turned_step(s, pairs)(i))),
            ],
            scratch_shapes=[
                pltpu.VMEM((length // QUERY_BLOCK, KEY_SPAN + QUERY_BLOCK, QUERY_BLOCK), F32),
                pltpu.VMEM((length, width), F32),
                pltpu.VMEM((length, width), F32),
            ],
        ),
        out_shape=[
            shape((3, length, pairs * width), BF16),
            shape((3, length, pairs * width // 2), BF16),
            shape((2, pairs * width), F32),
        ],
        compiler_params=settings(),
        cost_estimate=cost(5e9 * pairs, 1e6 * pairs),
        name="attend_backward",
    )(place, segs, segs_column, qkv, qkv, qkv, grads, lse)


ROW_BLOCK = 256
EARLY_BLOCK = 512


def row_stats(values):
    centre = jnp.mean(values, axis=-1, keepdims=True)
    shifted = values - centre
    spread = jnp.mean(shifted * shifted, axis=-1, keepdims=True)
    inverse = lax.rsqrt(spread + LN_EPS)
    return shifted * inverse, inverse, spread


def norm_back(upstream, scaled, inverse, gain_row):
    weighted = upstream * gain_row
    return inverse * (
        weighted
        - jnp.mean(weighted, axis=-1, keepdims=True)
        - scaled * jnp.mean(weighted * scaled, axis=-1, keepdims=True)
    )


def column_sum(values):
    return jnp.sum(values, axis=0, keepdims=True)


def accumulate(ref, values):
    step = pl.program_id(0)

    @pl.when(step == 0)
    def _():
        ref[...] = values

    @pl.when(step > 0)
    def _():
        ref[...] += values


def turn_kernel(g_ref, turned_ref, sum_ref):
    values = g_ref[...]
    turned_ref[...] = values.T
    accumulate(sum_ref, column_sum(values.astype(F32)))


def turn(cot):
    length, width = cot.shape
    return pl.pallas_call(
        turn_kernel,
        grid=(length // EARLY_BLOCK,),
        in_specs=[pl.BlockSpec((EARLY_BLOCK, width), lambda i: (i, 0))],
        out_specs=[
            pl.BlockSpec((width, EARLY_BLOCK), lambda i: (0, i)),
            pl.BlockSpec((1, width), lambda i: (0, 0)),
        ],
        out_shape=[shape((width, length), BF16), shape((1, width), F32)],
        compiler_params=settings(),
        cost_estimate=cost(0, 8e6),
        name="turn",
    )(cot)


def first_norm_kernel(x_ref, vec_ref, h_ref, turned_ref, scale_ref):
    scaled, _, spread = row_stats(x_ref[...].astype(F32))
    normed = (scaled * vec_ref[0:1, :] + vec_ref[1:2, :]).astype(BF16)
    h_ref[...] = normed
    turned_ref[...] = normed.T
    accumulate(scale_ref, jnp.broadcast_to(column_sum(jnp.sqrt(spread + LN_EPS)), (1, 128)))


def first_norm(rows, vec):
    length, width = rows.shape
    return pl.pallas_call(
        first_norm_kernel,
        grid=(length // EARLY_BLOCK,),
        in_specs=[
            pl.BlockSpec((EARLY_BLOCK, width), lambda i: (i, 0)),
            pl.BlockSpec(vec.shape, lambda i: (0, 0)),
        ],
        out_specs=[
            pl.BlockSpec((EARLY_BLOCK, width), lambda i: (i, 0)),
            pl.BlockSpec((width, EARLY_BLOCK), lambda i: (0, i)),
            pl.BlockSpec((1, 128), lambda i: (0, 0)),
        ],
        out_shape=[
            shape((length, width), BF16),
            shape((width, length), BF16),
            shape((1, 128), F32),
        ],
        compiler_params=settings(),
        cost_estimate=cost(0, 10e6),
        name="first_norm",
    )(rows, vec)


def weight_call(kernel, place, weights, grid, in_specs, operands, out_specs, out_shape, name, flops, moved, aliases=None, tile=None):
    arrays = [array for pieces, _ in weights for array, _ in pieces]

    def body(place_ref, *refs):
        at = len(arrays)
        ins = refs[at : at + len(operands)]
        at += len(operands)
        outs = refs[at : at + len(out_shape)]
        at += len(out_shape)
        buffers, sems = refs[at : at + len(weights)], refs[at + len(weights) :]

        copies, ref = [], 0
        for (pieces, _), buffer, sem in zip(weights, buffers, sems):
            first = 0
            for _, plan in pieces:
                copies.append(piece_copies(place_ref, refs[ref], plan, buffer, sem, first))
                ref += 1
                first += len(plan)

        @pl.when(pl.program_id(0) == 0)
        def _():
            for _, group in copies:
                for copy in group:
                    copy.start()
            if tile is None:
                for _, group in copies:
                    for copy in group:
                        copy.wait()

        if tile is not None:
            now = tile(place_ref, pl.program_id(0))
            for at, group in copies:

                @pl.when((pl.program_id(0) == 0) if at is None else (at // TILE == now))
                def _(group=group):
                    for copy in group:
                        copy.wait()

        kernel(place_ref, *ins, *outs, *buffers)

    return pl.pallas_call(
        body,
        grid_spec=pltpu.PrefetchScalarGridSpec(
            num_scalar_prefetch=1,
            grid=grid,
            in_specs=[pl.BlockSpec(memory_space=pltpu.HBM)] * len(arrays) + in_specs,
            out_specs=out_specs,
            scratch_shapes=[pltpu.VMEM((D, columns), BF16) for _, columns in weights]
            + [
                pltpu.SemaphoreType.DMA((sum(len(plan) for _, plan in pieces),))
                for pieces, _ in weights
            ],
        ),
        out_shape=out_shape,
        input_output_aliases={1 + len(arrays) + i: o for i, o in (aliases or {}).items()},
        compiler_params=settings(),
        cost_estimate=cost(flops, moved),
        name=name,
    )(place, *arrays, *operands)


TILE = 1024
GRADIENT_MIB = 57


def whole(array_shape):
    return pl.BlockSpec(array_shape, lambda i, *_: (0,) * len(array_shape))


def row_spec(width, block=ROW_BLOCK):
    return pl.BlockSpec((block, width), lambda i, *_: (i, 0))


def column_spec(height, tile=TILE):
    return pl.BlockSpec((height, tile), lambda i, *_: (0, i))


def tile_of(buffer, index):
    return buffer[:, pl.ds(pl.multiple_of(index * TILE, TILE), TILE)]


def split_spec(height, steps):
    return (
        pl.BlockSpec((height, TILE), lambda i, place: (0, turned_step(place, steps)(i))),
        pl.BlockSpec((height, TILE), lambda i, place: (0, jnp.minimum(i, steps // 2 - 1))),
    )


def project_kernel(place, h_ref, bias_ref, o_ref, buffer):
    o_ref[...] = (mxu(h_ref[...], tile_of(buffer, pl.program_id(0)), NN) + bias_ref[...]).astype(BF16)


def project(normed, bias, weight, place):
    length, width = normed.shape
    columns = bias.shape[1]
    return weight_call(
        project_kernel,
        place,
        [(weight, columns)],
        (columns // TILE,),
        [whole((length, width)), column_spec(1)],
        [normed, bias],
        [column_spec(length)],
        [shape((length, columns), BF16)],
        "project",
        2 * length * width * columns,
        16e6,
        tile=lambda place, i: i,
    )[0]


def join_kernel(place, c_ref, x_ref, vec_ref, middle_ref, h_ref, turned_ref, buffer):
    middle = (
        x_ref[...].astype(F32) + mxu(c_ref[...], buffer[...], NT) + vec_ref[4:5, :]
    )
    middle_ref[...] = middle
    normed = (row_stats(middle)[0] * vec_ref[5:6, :] + vec_ref[6:7, :]).astype(BF16)
    h_ref[...] = normed
    turned_ref[...] = normed.T


def join(context, rows, vec, weight, place):
    length, width = context.shape
    return weight_call(
        join_kernel,
        place,
        [(weight, D)],
        (length // ROW_BLOCK,),
        [row_spec(width), row_spec(D), whole(vec.shape)],
        [context, rows, vec],
        [row_spec(D), row_spec(D), pl.BlockSpec((D, ROW_BLOCK), lambda i, *_: (0, i))],
        [shape((length, D), F32), shape((length, D), BF16), shape((D, length), BF16)],
        "join",
        2 * length * width * D,
        16e6,
    )


def widen_kernel(place, h_ref, bias_ref, a_ref, slope_ref, send_ref, buffer):
    root, cubic = math.sqrt(2.0 / math.pi), 0.044715
    weights = tile_of(buffer, pl.program_id(0))
    for first in range(0, h_ref.shape[0], ROW_BLOCK):
        rows = slice(first, first + ROW_BLOCK)
        u = mxu(h_ref[rows, :], weights, NN) + bias_ref[...]
        square = u * u
        bent = jnp.tanh(u * (root + (root * cubic) * square))
        near = 0.5 + 0.5 * bent
        full = u * near
        low = full.astype(BF16)
        a_ref[rows, :] = low
        slope_ref[rows, :] = (
            near + full * (1.0 - near) * (2.0 * root + (6.0 * root * cubic) * square)
        ).astype(BF16)
        if send_ref is not None:
            send_ref[rows, :] = low


def widen_half(normed, bias, weight, place, before=()):
    length, width = normed.shape
    columns = bias.shape[1]
    steps = columns // TILE // 2

    def at(i, s):
        return (s[3] if before else 1 - s[3]) * steps + i

    full = pl.BlockSpec((length, TILE), lambda i, s: (0, at(i, s)))
    sends = [] if before else [pl.BlockSpec((length, TILE), lambda i, s: (0, i))]

    def kernel(place, h_ref, bias_ref, *refs):
        a_ref, slope_ref, *send, buffer = refs[len(before) :]
        widen_kernel(place, h_ref, bias_ref, a_ref, slope_ref, send[0] if send else None, buffer)

    return weight_call(
        kernel,
        place,
        [(weight, columns // 2)],
        (steps,),
        [whole((length, width)), pl.BlockSpec((1, TILE), lambda i, s: (0, at(i, s)))]
        + [pl.BlockSpec(memory_space=pltpu.HBM)] * len(before),
        [normed, bias, *before],
        [full, full] + sends,
        [shape((length, columns), BF16)] * 2 + [shape((length, columns // 2), BF16)] * len(sends),
        "widen",
        length * width * columns,
        14e6,
        {2: 0, 3: 1} if before else {},
    )


def hidden_back_kernel(steps, place, g_ref, slope_ref, o_ref, send_ref, sum_ref, buffer):
    step = pl.program_id(0)
    weights = tile_of(buffer, turned_step(place, steps)(step))
    total = jnp.zeros((1, TILE), F32)
    for first in range(0, g_ref.shape[0], ROW_BLOCK):
        rows = slice(first, first + ROW_BLOCK)
        grad = (mxu(g_ref[rows, :], weights, NN) * slope_ref[rows, :].astype(F32)).astype(BF16)
        o_ref[rows, :] = grad
        total = total + column_sum(grad.astype(F32))
    sum_ref[pl.ds(turned_step(place, steps)(step), 1), :] = total

    @pl.when(step < steps // 2)
    def _():
        send_ref[...] = o_ref[...]


def hidden_back(cot, slope, weight, place):
    length, width = cot.shape
    columns = slope.shape[1]
    steps = columns // TILE
    full, half = split_spec(length, steps)
    return weight_call(
        partial(hidden_back_kernel, steps),
        place,
        [(weight, columns)],
        (steps,),
        [whole((length, width)), full],
        [cot, slope],
        [full, half, whole((steps, TILE))],
        [
            shape((length, columns), BF16),
            shape((length, columns // 2), BF16),
            shape((steps, TILE), F32),
        ],
        "hidden_back",
        2 * length * width * columns,
        28e6,
        tile=lambda place, i: turned_step(place, steps)(i),
    )


def middle_back_kernel(
    place, gu_ref, x1_ref, g_ref, vec_ref, gx_ref, ga_ref, turned_ref, gc_ref, sums_ref, up, out
):
    upstream = mxu(gu_ref[...], up[...], NT)
    scaled, inverse, _ = row_stats(x1_ref[...])
    grad = g_ref[...].astype(F32) + norm_back(upstream, scaled, inverse, vec_ref[5:6, :])
    gx_ref[...] = grad
    low = grad.astype(BF16)
    ga_ref[...] = low
    turned_ref[...] = low.T
    gc_ref[...] = mxu(low, out[...], NN).astype(BF16)
    accumulate(
        sums_ref,
        jnp.concatenate(
            [
                column_sum(low.astype(F32)),
                column_sum(upstream * scaled),
                column_sum(upstream),
            ],
            axis=0,
        ),
    )


def middle_back(hidden_grad, middle, cot, vec, up, out, place):
    length, columns = hidden_grad.shape
    return weight_call(
        middle_back_kernel,
        place,
        [(up, columns), (out, D)],
        (length // ROW_BLOCK,),
        [row_spec(columns), row_spec(D), row_spec(D), whole(vec.shape)],
        [hidden_grad, middle, cot, vec],
        [
            row_spec(D),
            row_spec(D),
            pl.BlockSpec((D, ROW_BLOCK), lambda i, *_: (0, i)),
            row_spec(D),
            whole((3, D)),
        ],
        [
            shape((length, D), F32),
            shape((length, D), BF16),
            shape((D, length), BF16),
            shape((length, D), BF16),
            shape((3, D), F32),
        ],
        "middle_back",
        2 * length * D * (columns + D),
        36e6,
    )


def input_back_kernel(place, lower_ref, upper_ref, x_ref, gx_ref, vec_ref, o_ref, sums_ref, buffer):
    upstream = None
    for j in range(3):
        for part, ref in enumerate((lower_ref, upper_ref)):
            width = ref.shape[2]
            start = j * D + part * width
            piece = mxu(ref[j], buffer[:, start : start + width], NT)
            upstream = piece if upstream is None else upstream + piece
    scaled, inverse, _ = row_stats(x_ref[...].astype(F32))
    o_ref[...] = gx_ref[...] + norm_back(upstream, scaled, inverse, vec_ref[0:1, :])
    accumulate(
        sums_ref,
        jnp.concatenate([column_sum(upstream * scaled), column_sum(upstream)], axis=0),
    )


def input_back(lower, upper, rows, middle_grad, vec, weight, place):
    length = rows.shape[0]
    half = lower.shape[2]
    stacked = pl.BlockSpec((3, ROW_BLOCK, half), lambda i, *_: (0, i, 0))
    return weight_call(
        input_back_kernel,
        place,
        [(weight, 3 * D)],
        (length // ROW_BLOCK,),
        [stacked, stacked, row_spec(D), row_spec(D), whole(vec.shape)],
        [lower, upper, rows, middle_grad, vec],
        [row_spec(D), whole((2, D))],
        [shape((length, D), F32), shape((2, D), F32)],
        "input_back",
        2 * length * D * 3 * D,
        24e6,
    )


def narrow_kernel(place, a_ref, x1_ref, vec_ref, o_ref, buffer):
    o_ref[...] = x1_ref[...] + mxu(a_ref[...], buffer[...], NT) + vec_ref[11:12, :]


def narrow(active, middle, vec, weight, place):
    length, columns = active.shape
    return weight_call(
        narrow_kernel,
        place,
        [(weight, columns)],
        (length // ROW_BLOCK,),
        [row_spec(columns), row_spec(D), whole(vec.shape)],
        [active, middle, vec],
        [row_spec(D)],
        [shape((length, D), F32)],
        "narrow",
        2 * length * D * columns,
        26e6,
    )[0]


def gradient_kernel(cut, place, t_ref, t2_ref, r_ref, r2_ref, *refs):
    total = refs[-1]
    total[...] = (
        mxu(t_ref[...], r_ref[0], NN) + mxu(t2_ref[...], r2_ref[0], NN)
    ).astype(BF16)
    step, outs = pl.program_id(0), list(refs[:-1])
    z_count, _, rows, _ = outs[0].shape

    def share(send_ref, keep_ref, x_first):
        for z in range(z_count):
            for other in range(2):
                for ref, away in ((send_ref, True), (keep_ref, False)):
                    x = (1 - place[1] if away else place[1]) if x_first else other
                    y = other if x_first else (1 - place[2] if away else place[2])
                    first = pl.multiple_of(((2 * z + x) * 2 + y) * rows, rows)
                    ref[z, other] = total[pl.ds(first, rows), :]

    if cut:
        send, keep = outs[:2]
        outs = outs[2:]

        @pl.when(step < cut)
        def _():
            share(send, keep, True)

    if outs:

        @pl.when(step >= cut)
        def _():
            share(outs[0], outs[1], False)


def gradient(turned, turned_other, right, right_other, place, n_dp, x_tiles, tiles):
    groups, length, columns = right.shape
    half = columns // 2
    tile = groups * half // tiles
    steps = half // tile
    rows = D // n_dp // 2
    block = (n_dp // 2, 2, rows, tile)
    specs, shapes = [], []
    if x_tiles:
        specs += [pl.BlockSpec(block, lambda i, s: (0, 0, 0, jnp.minimum(i, x_tiles - 1)))] * 2
        shapes += [shape(block[:3] + (x_tiles * tile,), BF16)] * 2
    if x_tiles < tiles:
        specs += [pl.BlockSpec(block, lambda i, s: (0, 0, 0, jnp.maximum(i - x_tiles, 0)))] * 2
        shapes += [shape(block[:3] + ((tiles - x_tiles) * tile,), BF16)] * 2
    fixed = pl.BlockSpec((D, length), lambda i, s: (0, 0))
    return pl.pallas_call(
        partial(gradient_kernel, x_tiles),
        grid_spec=pltpu.PrefetchScalarGridSpec(
            num_scalar_prefetch=1,
            grid=(tiles,),
            in_specs=[
                fixed,
                fixed,
                pl.BlockSpec(
                    (1, length, tile),
                    lambda i, s: (i // steps, 0, s[3] * steps + lax.rem(i, steps)),
                ),
                pl.BlockSpec((1, length, tile), lambda i, s: (i // steps, 0, lax.rem(i, steps))),
            ],
            out_specs=specs,
            scratch_shapes=[pltpu.VMEM((D, tile), BF16)],
        ),
        out_shape=shapes,
        compiler_params=settings(GRADIENT_MIB),
        cost_estimate=cost(4 * D * length * groups * half, 14e6),
        name="gradient",
    )(place, turned, turned_other, right, right_other)


def wide_sum(*terms):
    return reduce(lambda a, b: a + b, [term.astype(F32) for term in terms])


def take(array, index, axis):
    return lax.dynamic_index_in_dim(array, index, axis, keepdims=False)


def near_free():
    return pl.CostEstimate(flops=1, bytes_accessed=1, transcendentals=0)


def assemble(place, arrays, shapes, moves):
    def body(place_ref, *refs):
        sems = refs[-1]
        copies = []
        for n, (source, at, target, to) in enumerate(moves):
            src, dst = refs[source], refs[len(arrays) + target]
            at = at(place_ref) if callable(at) else at
            copies.append(
                pltpu.make_async_copy(
                    src if at is None else src.at[at], dst if to is None else dst.at[to], sems.at[n]
                )
            )
        for copy in copies:
            copy.start()
        for copy in copies:
            copy.wait()

    return pl.pallas_call(
        body,
        grid_spec=pltpu.PrefetchScalarGridSpec(
            num_scalar_prefetch=1,
            grid=(1,),
            in_specs=[pl.BlockSpec(memory_space=pltpu.HBM)] * len(arrays),
            out_specs=[whole(dims) for dims in shapes],
            scratch_shapes=[pltpu.SemaphoreType.DMA((len(moves),))],
        ),
        out_shape=[shape(dims, BF16) for dims in shapes],
        compiler_params=settings(),
        cost_estimate=near_free(),
        name="assemble",
    )(place, *arrays)


def sums_of_two(place, pairs, axes):
    count = len(pairs)

    def body(place_ref, *refs):
        ins, outs = refs[: 2 * count], refs[2 * count : 3 * count]
        buffers, sems = refs[3 * count : 5 * count], refs[-1]
        copies = []
        for n in range(2 * count):
            away = 1 - place_ref[axes[n // 2]]
            copies.append(pltpu.make_async_copy(ins[n].at[:, away], buffers[n], sems.at[n]))
        for copy in copies:
            copy.start()
        for copy in copies:
            copy.wait()
        for n in range(count):
            kept, recv = buffers[2 * n], buffers[2 * n + 1]
            outs[n][...] = (kept[...].astype(F32) + recv[...].astype(F32)).astype(BF16)

    dims = [keep.shape[:1] + keep.shape[2:] for keep, _ in pairs]
    return pl.pallas_call(
        body,
        grid_spec=pltpu.PrefetchScalarGridSpec(
            num_scalar_prefetch=1,
            grid=(1,),
            in_specs=[pl.BlockSpec(memory_space=pltpu.HBM)] * (2 * count),
            out_specs=[whole(d) for d in dims],
            scratch_shapes=[pltpu.VMEM(d, BF16) for d in dims for _ in range(2)]
            + [pltpu.SemaphoreType.DMA((2 * count,))],
        ),
        out_shape=[shape(d, BF16) for d in dims],
        compiler_params=settings(),
        cost_estimate=near_free(),
        name="sums_of_two",
    )(place, *[array for pair in pairs for array in pair])


def sums_of_z(place, terms, axes, picks, recv=None):
    count = len(terms)
    widths = [keep.shape[3] for keep, _, _ in terms]
    rows, total = terms[0][0].shape[2], sum(widths)
    dtypes = [BF16, F32] if recv is not None else [BF16]
    dims = [(rows, total)] * 2 if recv is not None else [(len(picks), rows, total)]
    extra = [] if recv is None else [recv]

    def body(place_ref, *refs):
        ins = refs[: 3 * count]
        add = refs[3 * count : 3 * count + len(extra)]
        at = 3 * count + len(extra)
        outs, buffers, sems = refs[at : at + len(dims)], refs[at + len(dims) : -1], refs[-1]
        copies = []
        for p, (bits, _, _, _) in enumerate(picks):
            z = place_ref[0] ^ bits
            for n in range(3 * count):
                group, part = divmod(n, 3)
                source = ins[n].at[z] if part == 2 else ins[n].at[z, place_ref[axes[group]]]
                copies.append(
                    pltpu.make_async_copy(source, buffers[group].at[p, part], sems.at[len(copies)])
                )
        for copy in copies:
            copy.start()
        for copy in copies:
            copy.wait()
        for p, (_, added, out, row) in enumerate(picks):
            first = 0
            for group, width in enumerate(widths):
                columns = slice(first, first + width)
                first += width
                value = wide_sum(*[buffers[group][p, part] for part in range(3)])
                if added is not None:
                    value = value + add[0][added, :, columns].astype(F32)
                if row is None:
                    outs[out][:, columns] = value.astype(dtypes[out])
                else:
                    outs[out][row, :, columns] = value.astype(dtypes[out])

    return pl.pallas_call(
        body,
        grid_spec=pltpu.PrefetchScalarGridSpec(
            num_scalar_prefetch=1,
            grid=(1,),
            in_specs=[pl.BlockSpec(memory_space=pltpu.HBM)] * (3 * count)
            + [whole(array.shape) for array in extra],
            out_specs=[whole(d) for d in dims],
            scratch_shapes=[pltpu.VMEM((len(picks), 3, rows, width), BF16) for width in widths]
            + [pltpu.SemaphoreType.DMA((len(picks) * 3 * count,))],
        ),
        out_shape=[shape(d, dtype) for d, dtype in zip(dims, dtypes)],
        compiler_params=settings(),
        cost_estimate=near_free(),
        name="sums_of_z",
    )(place, *[array for term in terms for array in term], *extra)


def finish(halves, before=None):
    widths = [total.shape[1] for total, _ in halves]
    rows = halves[0][0].shape[0]
    extra = [] if before is None else [before]

    def body(*refs):
        out, squares = refs[-2:]
        result = refs[2 * len(halves)][...] if extra else jnp.zeros((1, 128), F32)
        first = 0
        for n, width in enumerate(widths):
            value = refs[2 * n][...] + refs[2 * n + 1][...].astype(F32)
            out[:, first : first + width] = value.astype(BF16)
            first += width
            result = result + jnp.sum(value * value)
        squares[...] = result

    return pl.pallas_call(
        body,
        out_shape=[shape((rows, sum(widths)), BF16), shape((1, 128), F32)],
        compiler_params=settings(),
        cost_estimate=near_free(),
        name="finish",
    )(*[array for half in halves for array in half], *extra)


def adam_step(weight, grad, first, second, rate, decay):
    first_next = BETA_ONE * first + (1.0 - BETA_ONE) * grad
    second_next = BETA_TWO * second + (1.0 - BETA_TWO) * grad * grad
    first_hat = first_next / (1.0 - BETA_ONE**STEP)
    second_hat = second_next / (1.0 - BETA_TWO**STEP)
    weight_next = weight - rate * (first_hat / (jnp.sqrt(second_hat) + ADAM_EPS) + decay * weight)
    return (weight_next, first_next, second_next)


def adam_kernel(halves, groups, place, factor, *refs):
    pieces, rest = refs[: 4 * groups], refs[4 * groups :]
    w_ref, m_ref, s_ref, wn_ref, mn_ref, sn_ref, half_ref = rest
    height, width = pieces[0].shape
    step = pl.program_id(0)

    def update(group, core, y, columns):
        choice = (core ^ place[3]) * 2 + (y ^ place[2])
        rows = slice(y * height, (y + 1) * height)
        grad = pieces[4 * group][...]
        for k in (1, 2, 3):
            grad = jnp.where(choice == k, pieces[4 * group + k][...], grad)
        new = adam_step(
            w_ref[rows, columns],
            grad.astype(F32) * factor[0],
            m_ref[rows, columns],
            s_ref[rows, columns],
            MATRIX_RATE,
            DECAY,
        )
        wn_ref[rows, columns], mn_ref[rows, columns], sn_ref[rows, columns] = new
        half_ref[rows, columns] = new[0].astype(BF16)

    for y in range(2):
        if halves == 1:
            update(0, step // 2, y, slice(None))
        else:
            for group in range(groups):

                @pl.when(lax.rem(step, groups) == group)
                def _(group=group):
                    for core in range(2):
                        update(group, core, y, slice(core * width, (core + 1) * width))


def adam(place, factor, pieces, starts, weight, first, second):
    rows, columns = weight.shape
    groups = len(starts)
    if groups == 1:
        steps, tile = 4, columns // 4
        width = tile
        specs = [
            pl.BlockSpec((rows // 2, width), lambda i, *_: (0, starts[0] // width + lax.rem(i, 2)))
        ] * 4
    else:
        steps, tile = columns // 512, 512
        width = tile // 2
        specs = [
            pl.BlockSpec(
                (rows // 2, width), lambda i, *_, start=start: (0, start // width + i // groups)
            )
            for start in starts
            for _ in range(4)
        ]
    block = pl.BlockSpec((rows, tile), lambda i, *_: (0, i))
    full = (rows, columns)
    return pl.pallas_call(
        partial(adam_kernel, tile // width, groups),
        grid_spec=pltpu.PrefetchScalarGridSpec(
            num_scalar_prefetch=2,
            grid=(steps,),
            in_specs=specs + [block] * 3,
            out_specs=[block] * 4,
        ),
        out_shape=[shape(full, F32)] * 3 + [shape(full, BF16)],
        compiler_params=settings(20),
        cost_estimate=cost(0, rows * columns * 28),
        name="adam",
    )(place, factor, *(pieces * groups), weight, first, second)


def tied(values, *others):
    return lax.optimization_barrier((values,) + others)[0]


KERNELS = (
    turn,
    first_norm,
    project,
    attend_forward,
    join,
    widen_half,
    hidden_back,
    middle_back,
    attend_backward,
    gradient,
    input_back,
    narrow,
)


class Order:
    def __init__(self):
        self.last = []
        self.pending = []

    def __call__(self, work, *operands):
        if self.last:
            leaves, tree = jax.tree_util.tree_flatten(operands)
            arrays = [leaf for leaf in leaves if isinstance(leaf, jax.Array)]
            if work in KERNELS:
                arrays[0] = tied(arrays[0], *self.last, *self.pending)
            else:
                arrays = lax.optimization_barrier((*arrays, *self.last, *self.pending))
            arrays = iter(arrays)
            leaves = [next(arrays) if isinstance(leaf, jax.Array) else leaf for leaf in leaves]
            operands = jax.tree_util.tree_unflatten(tree, leaves)
        result = work(*operands)
        self.last, self.pending = jax.tree_util.tree_leaves(result), []
        return result

    def send(self, array, **bits):
        return swap(tied(array, *self.last), **bits)

    def land(self, *arrays):
        self.pending += arrays

    def cross(self, array):
        crossed = swap(tied(array, *self.last, *self.pending), core=1)
        return crossed

    def cross_all(self, *arrays):
        crossed = [self.cross(array) for array in arrays]
        self.pending += crossed
        return crossed


def stack_z(*parts):
    return jnp.stack(parts)


def to_send(own, place, parts, split_y, extra=None):
    mine = pack(own, place, parts, split_y).astype(BF16)
    if extra is None:
        return mine
    flat = extra.astype(BF16).reshape(-1, mine.shape[1])
    spare = -(mine.shape[0] + flat.shape[0]) % 16
    return jnp.concatenate([mine, flat, jnp.zeros((spare, mine.shape[1]), BF16)], axis=0)


def vectors_of(near, far, index, rows, dims, n_dp):
    count = dims[0] * dims[1] // near.shape[2]
    both = jnp.stack([near[:, rows : rows + count], far[:, rows : rows + count]], axis=1)
    both = both.reshape((n_dp,) + dims)
    return jnp.concatenate([take(both, index ^ j, 0) for j in range(n_dp)], axis=1).astype(F32)


def per_device(
    tokens,
    segment_ids,
    cotangent,
    qkv_weight,
    out_weight,
    up_weight,
    down_weight,
    vectors,
    qkv_first,
    qkv_second,
    out_first,
    out_second,
    up_first,
    up_second,
    down_first,
    down_second,
    vectors_first,
    vectors_second,
):
    n_dp, n_rep = lax.axis_size("dp"), lax.axis_size("rep")
    paired = n_dp == 8 and n_rep == 4
    dp, rep = lax.axis_index("dp"), lax.axis_index("rep")
    z, x, y, core = dp // 2, dp % 2, rep // 2, rep % 2
    place = jnp.stack([z, x, y, core]).astype(jnp.int32)
    seq_len = tokens.shape[1]
    segs_column = segment_ids.reshape(seq_len, 1)
    rows = tokens.reshape(seq_len, D)
    cot = cotangent.reshape(seq_len, D)
    up_rows = FF // D
    shard = qkv_weight.shape[0]
    masters = (qkv_weight, out_weight, up_weight, down_weight, vectors)
    pairs = HEADS // 2
    run = Order()

    if paired:

        def held(zs, here, x=0, y=0, there=None):
            return [(here, zs, x, y, 0), (there, zs, x, y, 1)]

        def all_z(mine):
            return [run.send(mine, z=bits) for bits in (1, 2, 3)]

        half, b_two = FF // 2, 3 * D // 4
        straight, zs = (0, 1, 2, 3), (0, 2, 1, 3)
        mine_b = to_send(qkv_weight, place, [(0, D, D // 2)], True, vectors)
        near_b = [swap(mine_b, z=bits) for bits in (1, 2, 3)]
        run.last = [mine_b]
        mine_a = run(to_send, qkv_weight, place, [(2 * D, D // 2, D // 2)], False)
        mine_two = run(
            lambda up, out: jnp.concatenate(
                [
                    pack(up, place, [(D // 2, half, b_two)], True),
                    pack(out, place, [(0, D // 2, D // 2)], False),
                ],
                axis=1,
            ).astype(BF16),
            up_weight,
            out_weight,
        )
        mine_three = run(to_send, down_weight, place, [(0, half, half // 2)], True)
        mine_last = run(to_send, up_weight, place, [(0, half, D // 2)], False)
        stack_b = run(stack_z, mine_b, *near_b)
        far_b, side_b = run.send(stack_b, x=1), run.send(stack_b, y=1)
        near_a = all_z(mine_a)
        cot_turned, down_bias_grad = run(turn, cot)
        run.land(far_b, side_b)
        vec = run(vectors_of, stack_b, far_b, dp, shard, vectors.shape, n_dp)
        across_b = run.send(far_b, y=1)
        stack_a = run(stack_z, mine_a, *near_a)
        far_a, far_two = run.send(stack_a, x=1), run.send(mine_two, z=2)
        near_b_other, far_b_other = run.send(stack_b, core=1), run.send(far_b, core=1)
        normed_one, normed_one_turned, scale_sum = run(first_norm, rows, vec)
        run.land(near_b_other, far_b_other, across_b, far_a, far_two)
        side_b_other, across_b_other, near_a_other, far_a_other = run.cross_all(
            side_b, across_b, stack_a, far_a
        )
        pair_two = run(stack_z, mine_two, far_two)
        other_two = run.send(pair_two, z=1)
        normed_one_turned_other = run.send(normed_one_turned, core=1)
        cot_turned_other = run.send(cot_turned, core=1)
        qkv_all = gathered(
            shard,
            held(straight, stack_b, there=near_b_other)
            + held(straight, far_b, 1, there=far_b_other)
            + held(straight, side_b, 0, 1, side_b_other)
            + held(straight, across_b, 1, 1, across_b_other),
            0,
            D // 2,
            0,
            D,
            D // 2,
        ) + gathered(
            shard,
            held(straight, stack_a, there=near_a_other) + held(straight, far_a, 1, there=far_a_other),
            0,
            D // 2,
            2 * D,
            D // 2,
            0,
        )
    else:
        vec = lax.all_gather(vectors.astype(BF16), "dp", axis=1, tiled=True).astype(F32)
        low = qkv_weight.astype(BF16)
        qkv_all = whole_rows(low)
        out_all, up_all, down_all = (
            whole_rows(own.astype(BF16)) for own in (out_weight, up_weight, down_weight)
        )
        cot_turned, down_bias_grad = run(turn, cot)
        normed_one, normed_one_turned, scale_sum = run(first_norm, rows, vec)

    qkv_bias = jnp.concatenate([vec[2:3], jnp.zeros((1, D), F32), vec[3:4]], axis=1)
    qkv = run(project, normed_one, qkv_bias, qkv_all, place)
    if paired:
        run.land(normed_one_turned_other, cot_turned_other)
        stack_b, stack_a = run(
            lambda *t: assemble(
                place,
                t,
                [(4, shard, b_two), (4, shard, D // 2)],
                [
                    (n, (slice(0, 2), slice(None), columns), out, slice(2 * n, 2 * n + 2))
                    for n in range(2)
                    for out, columns in ((0, slice(0, b_two)), (1, slice(b_two, b_two + D // 2)))
                ],
            ),
            pair_two,
            other_two,
        )
        far_b, side_b = run.send(stack_b, x=1), run.send(stack_b, y=1)
        far_last, far_three = run.send(mine_last, z=2), run.send(mine_three, z=2)
        near_a_other = run.send(stack_a, core=1)
    context, lower_sums = run(attend_forward, qkv, segment_ids, segs_column, 0, pairs // 2)
    if paired:
        run.land(far_b, side_b, near_a_other)
        pair_last, pair_three = run(
            lambda *t: assemble(
                place,
                t,
                [(2, shard, D // 2), (2, shard, half // 2)],
                [(n, None, n // 2, n % 2) for n in range(4)],
            ),
            mine_last,
            far_last,
            mine_three,
            far_three,
        )
        across_b, far_a = run.send(far_b, y=1), run.send(stack_a, x=1)
        other_last, other_three = run.send(pair_last, z=1), run.send(pair_three, z=1)
        near_b_other = run.send(stack_b, core=1)
    context, upper_sums = run(attend_forward, qkv, segment_ids, segs_column, pairs // 2, pairs // 2, context)
    if paired:
        run.land(across_b, far_a, near_b_other, other_last, other_three)
        [far_a_other] = run.cross_all(far_a)

        def other_half(s):
            start = pl.multiple_of((1 - s[3]) * (D // 2), D // 2)
            return (slice(None), pl.ds(start, D // 2))

        stack_last, stack_three, context_send = run(
            lambda *t: assemble(
                place,
                t,
                [(4, shard, D // 2), (4, shard, half // 2), (seq_len, D // 2)],
                [(n, None, n // 2, slice(n % 2 * 2, n % 2 * 2 + 2)) for n in range(4)]
                + [(4, other_half, 2, None)],
            ),
            pair_last,
            other_last,
            pair_three,
            other_three,
            context,
        )
        a_held = held(zs, stack_a, there=near_a_other) + held(zs, far_a, 1, there=far_a_other)
        out_all = gathered(shard, a_held, 0, D // 2, 0, D // 2, 0)
        far_last = run.send(stack_last, x=1)
        side_b_other, far_b_other = run.send(side_b, core=1), run.send(far_b, core=1)
        across_b_other, near_last_other = run.send(across_b, core=1), run.send(stack_last, core=1)
    middle, normed_two, normed_two_turned = run(join, context, rows, vec, out_all, place)
    up_bias = vec[7 : 7 + up_rows].reshape(1, FF)
    if paired:
        run.land(side_b_other, far_b_other, across_b_other, near_last_other, far_last)
        [far_last_other] = run.cross_all(far_last)
        far_three, side_three = run.send(stack_three, x=1), run.send(stack_three, y=1)
        normed_two_turned_other = run.send(normed_two_turned, core=1)
        context_other = run.send(context_send, core=1)
        near_three_other = run.send(stack_three, core=1)
        b_held = (
            held(zs, stack_b, there=near_b_other)
            + held(zs, far_b, 1, there=far_b_other)
            + held(zs, side_b, 0, 1, side_b_other)
            + held(zs, across_b, 1, 1, across_b_other)
        )
        last_held = held(zs, stack_last, there=near_last_other) + held(
            zs, far_last, 1, there=far_last_other
        )
        def up_of(b_held, last_held, core_step):
            return gathered(shard, b_held, 0, b_two, D // 2, core_step, b_two) + gathered(
                shard, last_held, 0, D // 2, 0, core_step, 0
            )

        up_all = up_of(b_held, last_held, half)
        up_there, up_here = (
            up_of([t for t in b_held if t[4] == c], [t for t in last_held if t[4] == c], 0)
            for c in (1, 0)
        )
    else:
        up_there, up_here = (
            [(lax.dynamic_slice_in_dim(up_all[0][0], c * (FF // 2), FF // 2, 1), [up_all[0][1][0][:6] + (FF // 2, 0, 0, 0)])]
            for c in (1 - core, core)
        )
    active, slope, active_send = run(widen_half, normed_two, up_bias, up_there, place)
    if paired:
        run.land(far_three, side_three, normed_two_turned_other, context_other, near_three_other)
        across_three = run.send(far_three, y=1)
        active_other = run.send(active_send, core=1)
        far_three_other, side_three_other = run.send(far_three, core=1), run.send(side_three, core=1)
    active, slope = run(widen_half, normed_two, up_bias, up_here, place, (active, slope))

    if not paired:

        def product(turned, right):
            groups = [
                jnp.dot(turned, right[g], preferred_element_type=F32) for g in range(right.shape[0])
            ]
            return jnp.concatenate(groups, axis=1)

        grad_down = product(cot_turned, active[None])
        hidden_grad, _, up_bias_grad = hidden_back(cot, slope, down_all, place)
        grad_up = product(normed_two_turned, hidden_grad[None])
        middle_grad, branch_grad, branch_turned, context_grad, middle_sums = middle_back(
            hidden_grad, middle, cot, vec, up_all, out_all, place
        )
        grad_out = product(branch_turned, context[None])
        lower, _, lower_bias = attend_backward(
            qkv, segment_ids, segs_column, context_grad, lower_sums, 0, pairs // 2, place
        )
        upper, _, upper_bias = attend_backward(
            qkv, segment_ids, segs_column, context_grad, upper_sums, pairs // 2, pairs // 2, place
        )
        parts = [product(normed_one_turned, grads) for grads in (lower, upper)]
        parts = [[part[:, j * D // 2 : (j + 1) * D // 2] for j in range(3)] for part in parts]
        grad_qkv = jnp.concatenate([t for pair in zip(*parts) for t in pair], axis=1)
    else:


        def cut(turned, right, x_tiles, tiles):
            outs = run(gradient, *turned, *right, place, n_dp, x_tiles, tiles)
            parts = []
            if x_tiles:
                parts.append((outs[1], run.send(outs[0], x=1), 2, {"y": 1}))
            if x_tiles < tiles:
                parts.append((outs[-1], run.send(outs[-2], y=1), 1, {"x": 1}))
            return parts

        def cut_again(parts):
            sends = run(
                lambda pairs: sums_of_two(place, pairs, [part[2] for part in parts]),
                [part[:2] for part in parts],
            )
            return [
                (keep, recv, run.send(send, **way), axis)
                for (keep, recv, axis, way), send in zip(parts, sends)
            ]

        def along_z(terms):
            axes = [term[3] for term in terms]
            [send] = run(
                lambda t: sums_of_z(place, t, axes, [(1, None, 0, 0), (3, None, 0, 1)]),
                [term[:3] for term in terms],
            )
            return terms, run.send(send, z=1)

        def along_z_again(terms, recv):
            axes = [term[3] for term in terms]
            send, total = run(
                lambda t, r: sums_of_z(place, t, axes, [(2, 1, 0, None), (0, 0, 1, None)], r),
                [term[:3] for term in terms],
                recv,
            )
            return total, run.send(send, z=2)

        run.land(active_other, far_three_other, side_three_other)
        cut_down = cut((cot_turned, cot_turned_other), (active[None], active_other[None]), 1, 2)
        run.land(across_three)
        [across_three_other] = run.cross_all(across_three)
        down_all = gathered(
            shard,
            held(zs, stack_three, there=near_three_other)
            + held(zs, far_three, 1, there=far_three_other)
            + held(zs, side_three, 0, 1, side_three_other)
            + held(zs, across_three, 1, 1, across_three_other),
            0,
            FF // 4,
            0,
            half,
            FF // 4,
        )
        hidden_grad, hidden_send, up_bias_grad = run(hidden_back, cot, slope, down_all, place)
        terms_down = cut_again(cut_down)
        hidden_other = run.send(hidden_send, core=1)
        middle_grad, branch_grad, branch_turned, context_grad, middle_sums = run(
            middle_back, hidden_grad, middle, cot, vec, up_all, out_all, place
        )
        run.land(hidden_other)
        z_down = along_z(terms_down)
        branch_turned_other = run.send(branch_turned, core=1)
        cut_up = cut(
            (normed_two_turned, normed_two_turned_other), (hidden_grad[None], hidden_other[None]), 1, 2
        )
        run.land(branch_turned_other)
        half_down = along_z_again(*z_down)
        lower, lower_send, lower_bias = run(
            attend_backward, qkv, segment_ids, segs_column, context_grad, lower_sums, 0, pairs // 2, place
        )
        run.land(half_down[1])
        terms_up = cut_again(cut_up)
        lower_other = run.send(lower_send, core=1)
        cut_out = cut((branch_turned, branch_turned_other), (context[None], context_other[None]), 0, 1)
        run.land(lower_other)
        upper, upper_send, upper_bias = run(
            attend_backward,
            qkv,
            segment_ids,
            segs_column,
            context_grad,
            upper_sums,
            pairs // 2,
            pairs // 2,
            place,
        )
        terms_out = cut_again(cut_out)
        upper_other = run.send(upper_send, core=1)
        turned_pair = (normed_one_turned, normed_one_turned_other)
        cut_lower = cut(turned_pair, (lower, lower_other), 1, 3)
        run.land(terms_out[0][2], upper_other)
        cut_upper = cut(turned_pair, (upper, upper_other), 2, 3)
        z_up = along_z(terms_up)
    input_grad, input_sums = run(
        input_back, lower, upper, rows, middle_grad, vec, qkv_all, place
    )
    grad_vec = jnp.concatenate(
        [
            input_sums,
            jnp.concatenate([lower_bias, upper_bias], axis=1),
            middle_sums,
            up_bias_grad.reshape(up_rows, D),
            down_bias_grad,
            jnp.broadcast_to(scale_sum[:, :1], (1, D)),
        ],
        axis=0,
    )
    if paired:
        run.land(*[part[1] for part in cut_lower + cut_upper])
        [vec_recv] = run.cross_all(grad_vec)
        grad_vec = grad_vec + vec_recv
        terms_last = cut_again(cut_lower + cut_upper)
        half_up = along_z_again(*z_up)
    if paired:
        z_late = along_z(terms_out + terms_last)
        vec_recv = run.send(grad_vec, y=1)
    block_out = run(narrow, active, middle, vec, down_all, place)
    if paired:
        early, squares = run(finish, [half_down, half_up])
        early_other = run.send(early, y=1)
        half_late = along_z_again(*z_late)
        for bits in ({"x": 1}, {"z": 1}):
            grad_vec = run(lambda a, b: a + b, grad_vec, vec_recv)
            vec_recv = run.send(grad_vec, **bits)
        grad_vec = run(lambda a, b: a + b, grad_vec, vec_recv)
        vec_recv = run.send(grad_vec, z=2)
    total_rows = seq_len * n_dp * n_rep
    firsts = (qkv_first, out_first, up_first, down_first)
    seconds = (qkv_second, out_second, up_second, down_second)
    if paired:
        late, squares = run(finish, [half_late], squares)
        squares = squares + swap(squares, core=1)
        squares = squares + swap(squares, y=1)
        late_other = swap(tied(late, squares), y=1)
        for bits in ({"x": 1}, {"z": 1}, {"z": 2}):
            squares = squares + swap(squares, **bits)
        squares = squares[0, 0]
        grad_vec = grad_vec + vec_recv
    else:
        shards = [
            lax.psum(lax.psum_scatter(grad, "dp", scatter_dimension=0, tiled=True), "rep")
            for grad in (grad_qkv, grad_out, grad_up, grad_down)
        ]
        grad_vec = lax.psum(grad_vec, AXES)
        squares = lax.psum(reduce(lambda a, b: a + b, [jnp.sum(p * p) for p in shards]), "dp")
    input_scale = grad_vec[12, 0] / total_rows
    grad_vec = grad_vec[:12]
    grad_norm = jnp.sqrt(squares + jnp.sum(grad_vec * grad_vec))
    clip_factor = jnp.minimum(1.0, CLIP_NORM / (grad_norm + 1e-06))
    updates = []
    if paired:
        early = [early, early_other, swap(early, core=1), swap(early_other, core=1)]
        late = [late, late_other, swap(late, core=1), swap(late_other, core=1)]
        factor = clip_factor.reshape(1)
        sources = [
            (late, [D // 2, D // 2 + 3 * D // 4]),
            (late, [0]),
            (early, [half]),
            (early, [0]),
        ]
        for (pieces, starts), weight, first, second in zip(sources, masters, firsts, seconds):
            updates.append(adam(place, factor, pieces, starts, weight, first, second))
    else:
        for grad, weight, first, second in zip(shards, masters, firsts, seconds):
            new = adam_step(weight, grad * clip_factor, first, second, MATRIX_RATE, DECAY)
            updates.append(new + (new[0].astype(BF16),))
    width = vectors.shape[1]
    vec_shard = lax.dynamic_slice_in_dim(grad_vec, dp * width, width, 1)
    new = adam_step(
        vectors, vec_shard * clip_factor, vectors_first, vectors_second, VECTOR_RATE, 0.0
    )
    updates.append(new + (new[0].astype(BF16),))
    return (
        (
            block_out.reshape(1, seq_len, D),
            input_grad.reshape(1, seq_len, D),
            grad_norm,
            input_scale,
        )
        + tuple(update[0] for update in updates)
        + tuple(update[1] for update in updates)
        + tuple(update[2] for update in updates)
        + tuple(update[3] for update in updates)
    )


def solution(mesh):
    rows = P(("dp", "rep"), None, None)
    matrix, vector = P("dp", None), P(None, "dp")
    weights = (matrix,) * 4 + (vector,)
    return jax.shard_map(
        per_device,
        mesh=mesh,
        in_specs=(rows, P(("dp", "rep"), None), rows)
        + weights
        + (matrix,) * 8
        + (vector,) * 2,
        out_specs=(rows, rows, P(), P()) + weights * 4,
        check_vma=False,
    )
```
